128 devices in a mesh: row: 8 (over y_lo, x), col: 16 (over z, y_hi, core).
Axes of the slice: x: 4, y: 4 (y_hi: 2, y_lo: 2; y = y_hi * 2 + y_lo), z: 4, core: 2. Of those that a mesh axis runs over, the one named last changes fastest.
Arguments:
- latents: bfloat16 [2, 512, 1024, 128], P(None, 'row', 'col'), may hold values from -6 to 6
- timesteps: int32 [2], replicated, may hold values from 0 to 999
- time_table: float32 [1000, 128], replicated, may hold values from -6 to 6
- conv_fine: bfloat16 [3, 3, 128, 128], replicated, may hold values from -0.1875 to 0.1875
- conv_coarse: bfloat16 [3, 3, 128, 256], replicated, may hold values from -0.1875 to 0.1875
- lift: float32 [256, 128], replicated, may hold values from -0.375 to 0.375
- cotangent: bfloat16 [2, 512, 1024, 128], P(None, 'row', 'col'), may hold values from -6 to 6
Outputs:
- latent_grad: float32 [2, 512, 1024, 128], P(None, 'row', 'col')
- fine_kernel_grad: float32 [3, 3, 128, 128], replicated
- coarse_kernel_grad: float32 [3, 3, 128, 256], replicated
- lift_grad: float32 [256, 128], replicated
- table_grad: float32 [1000, 128], replicated
The draws below stay inside these ranges and needn't reach their ends.
All inputs are finite; a program needn't handle non-finite values.
Results may differ from the reference program's by a relative error of at most 0.014.
Values may be sent and summed in bfloat16 or wider, within the bound.
A program may use at most 128 MiB of HBM per device.

```python
import math
import jax
import jax.numpy as jnp
from jax import lax

CH_FINE = 128
CH_COARSE = 256
STEPS = 1000
LATENTS = 2
HEIGHT = 512
WIDTH = 1024


def block_levels(own_key, shape, split, smallest, largest):
    gain, own = 1.0, jax.random.fold_in(own_key, 6)
    for axis_at, shards_of in split:
        heights = jnp.exp(jax.random.uniform(jax.random.fold_in(own, axis_at), (shards_of,), jnp.float32, smallest / len(split), largest / len(split)))
        gain = gain * jnp.repeat(heights, shape[axis_at] // shards_of).reshape([-1 if axis == axis_at else 1 for axis in range(len(shape))])
    return gain


def normal_values(stream_key, dims, width, most, split=(), kind=jnp.bfloat16):
    result = jax.random.normal(stream_key, dims, jnp.float32) * width
    if len(split) > 0:
        result = block_levels(stream_key, dims, split, -0.22, 0.18) * result
    return jnp.clip(result, min=-most, max=most).astype(kind)


def setup_inputs(seed: int = 0) -> dict:
    streams_of = jax.random.split(jax.random.key(seed), 8)
    latents = normal_values(streams_of[0], (LATENTS, HEIGHT, WIDTH, CH_FINE), 1.0, 6.0, ((1, 8), (2, 16)))
    timesteps = jax.random.randint(streams_of[1], (LATENTS,), 0, STEPS).astype(jnp.int32)
    time_table = normal_values(streams_of[2], (STEPS, CH_FINE), 1.0, 6.0, (), jnp.float32)
    conv_fine = normal_values(streams_of[3], (3, 3, CH_FINE, CH_FINE), (9 * CH_FINE) ** -0.5, 0.1875)
    conv_coarse = normal_values(streams_of[4], (3, 3, CH_FINE, CH_COARSE), (9 * CH_FINE) ** -0.5, 0.1875)
    lift = normal_values(streams_of[5], (CH_COARSE, CH_FINE), CH_COARSE ** -0.5, 0.375, (), jnp.float32)
    cotangent = normal_values(streams_of[6], (LATENTS, HEIGHT, WIDTH, CH_FINE), 1.0, 6.0, ((1, 8), (2, 16)))
    return dict(latents=latents, timesteps=timesteps, time_table=time_table, conv_fine=conv_fine, conv_coarse=conv_coarse, lift=lift, cotangent=cotangent)


def conv_same(field_in, kernel):
    return lax.conv_general_dilated(field_in.astype(jnp.float32), kernel.astype(jnp.float32), (1, 1), ((1, 1), (1, 1)), dimension_numbers=('NHWC', 'HWIO', 'NHWC'), precision=lax.Precision.HIGHEST)

def conv_back(grad_in, kernel):
    flipped = jnp.transpose(kernel[::-1, ::-1], (0, 1, 3, 2))
    return conv_same(grad_in, flipped)

def kernel_grad(field_in, grad_in):
    padded = jnp.pad(field_in.astype(jnp.float32), ((0, 0), (1, 1), (1, 1), (0, 0)))
    grad_wide = grad_in.astype(jnp.float32)
    tile_rows, tile_cols = (grad_in.shape[1], grad_in.shape[2])
    pieces = []
    for row_tap in range(3):
        for col_tap in range(3):
            window = padded[:, row_tap:row_tap + tile_rows, col_tap:col_tap + tile_cols]
            pieces.append(jnp.einsum('bhwc,bhwd->cd', window, grad_wide, precision=lax.Precision.HIGHEST))
    return jnp.stack(pieces).reshape(3, 3, field_in.shape[3], grad_in.shape[3])

def silu_slope(values):
    logistic = jax.nn.sigmoid(values)
    return logistic * (1.0 + values * (1.0 - logistic))

def block_sum(field_in):
    count, tall, broad, chans = field_in.shape
    return field_in.astype(jnp.float32).reshape(count, tall // 2, 2, broad // 2, 2, chans).sum(axis=(2, 4))

def upsample(field_in):
    return jnp.repeat(jnp.repeat(field_in, 2, axis=1), 2, axis=2)

def reference(latents, timesteps, time_table, conv_fine, conv_coarse, lift, cotangent):
    onehot = (timesteps[:, None] == jnp.arange(STEPS, dtype=jnp.int32)[None, :]).astype(jnp.float32)
    embedding = jnp.dot(onehot, time_table, precision=lax.Precision.HIGHEST)
    pre_fine = conv_same(latents, conv_fine) + embedding[:, None, None, :]
    hidden = jax.nn.silu(pre_fine).astype(jnp.bfloat16)
    pooled = (0.25 * block_sum(hidden)).astype(jnp.bfloat16)
    pre_coarse = conv_same(pooled, conv_coarse)
    coarse_act = jax.nn.silu(pre_coarse).astype(jnp.bfloat16)
    up_grad = block_sum(cotangent)
    lift_sum = jnp.einsum('bhwc,bhwd->cd', coarse_act.astype(jnp.float32), up_grad, precision=lax.Precision.HIGHEST)
    coarse_back = jnp.einsum('bhwd,cd->bhwc', up_grad, lift, precision=lax.Precision.HIGHEST)
    grad_coarse = (coarse_back * silu_slope(pre_coarse)).astype(jnp.bfloat16)
    coarse_sum = kernel_grad(pooled, grad_coarse)
    pooled_grad = conv_back(grad_coarse, conv_coarse)
    hidden_grad = cotangent.astype(jnp.float32) + 0.25 * upsample(pooled_grad)
    grad_fine = (hidden_grad * silu_slope(pre_fine)).astype(jnp.bfloat16)
    fine_sum = kernel_grad(latents, grad_fine)
    latent_sum = grad_fine.astype(jnp.float32).sum(axis=(1, 2))
    table_sum = jnp.dot(onehot.T, latent_sum, precision=lax.Precision.HIGHEST)
    latent_grad = conv_back(grad_fine, conv_fine)
    factor = 1.0 / math.sqrt(LATENTS * HEIGHT * WIDTH)
    return (latent_grad, factor * fine_sum, factor * coarse_sum, factor * lift_sum, factor * table_sum)
```

```python
import functools
import math

import jax
import jax.numpy as jnp
from jax import lax
from jax.experimental import pallas as pl
from jax.experimental.pallas import tpu as pltpu
from jax.sharding import PartitionSpec as P

MESH = pl.DeviceIdType.MESH
f32 = jnp.float32
bf16 = jnp.bfloat16


def dot(a, b):
    return jnp.dot(a, b, preferred_element_type=f32)


def sigmoid(v):
    return 0.5 + 0.5 * jnp.tanh(0.5 * v)


def shifted(v, column, step):
    n = v.shape[1]
    ids = lax.broadcasted_iota(jnp.int32, v.shape, 1)
    edge = 0 if step == 1 else n - 1
    return jnp.where(ids == edge, column[:, None, :], pltpu.roll(v, step % n, 1))


def kernel(
    sizes,
    times, lat_in, cot_in, table_in, fine_in, coarse_in, lift_in,
    grad_out, fine_out, coarse_out, lift_out, table_out,
    lat, cot, table, kfine, kcoarse, lift, wide,
    w_fwd, w_back, wc_back, lift_hi, lift_lo,
    V, C2, SL, PO, UG, ACT, GC, G, VT, PT, OUT,
    sc_v, rc_v, sc_p, rc_p, sc_c, rc_c, sc_g, rc_g,
    a_send, a_r1, a_s2, a_r2, a_t, a_g, a_f,
    b_send, b_r1, b_s2, b_r2, b_t, b_g, b_f,
    l_send, l_r1, l_s2, l_r2,
    in_sem, out_sem, h_ssem, h_rsem, a_ssem, a_rsem, b_ssem, b_rsem, l_ssem, l_rsem,
):
    nr, nc, factor = sizes
    row, col = lax.axis_index("row"), lax.axis_index("col")
    up, down = lax.rem(row + nr - 1, nr), lax.rem(row + 1, nr)
    left, right = lax.rem(col + nc - 1, nc), lax.rem(col + 1, nc)
    count, tall, half = C2.shape[0], C2.shape[1], C2.shape[2]
    low = tall // 2
    chans = lat.shape[3]

    barrier = pltpu.get_barrier_semaphore()
    partners = [(lax.rem(row + d, nr), col) for d in range(1, nr)]
    partners += [(row, lax.rem(col + d, nc)) for d in range(1, nc)]
    partners += [(up, left), (up, right), (down, left), (down, right)]
    for who in partners:
        pl.semaphore_signal(barrier, inc=1, device_id=who, device_id_type=MESH)

    loads = {}
    pairs = [(lat_in.at[b], lat.at[b]) for b in range(count)]
    pairs += [(fine_in, kfine), (table_in, table)]
    pairs += [(cot_in.at[b], cot.at[b]) for b in range(count)]
    pairs += [(coarse_in, kcoarse), (lift_in, lift)]
    names = ["lat0", "lat1", "kfine", "table", "cot0", "cot1", "kcoarse", "lift"]
    for at, (src, dst) in enumerate(pairs):
        loads[names[at]] = pltpu.make_async_copy(src, dst, in_sem.at[at])
        loads[names[at]].start()

    def exchange(kind, b, buf, n, lo, hi, sc, rc):
        top, bottom = (row, col), None
        first = (kind * count + b) * 8
        first_col, last_col = sc.at[b, 0], sc.at[b, 1]
        to_left, to_right = rc.at[b, 1], rc.at[b, 0]
        lanes = pl.ds(lo, hi - lo)
        plan = [
            (buf.at[b, 1, :, lanes], buf.at[b, n + 1, :, lanes], (up, col)),
            (buf.at[b, n, :, lanes], buf.at[b, 0, :, lanes], (down, col)),
            (first_col, to_left.at[pl.ds(8, n)], (row, left)),
            (last_col, to_right.at[pl.ds(8, n)], (row, right)),
            (first_col.at[pl.ds(0, 8)], to_left.at[pl.ds(n + 8, 8)], (up, left)),
            (last_col.at[pl.ds(0, 8)], to_right.at[pl.ds(n + 8, 8)], (up, right)),
            (first_col.at[pl.ds(n - 8, 8)], to_left.at[pl.ds(0, 8)], (down, left)),
            (last_col.at[pl.ds(n - 8, 8)], to_right.at[pl.ds(0, 8)], (down, right)),
        ]
        return [
            pltpu.make_async_remote_copy(
                src_ref=src, dst_ref=dst, send_sem=h_ssem.at[first + at], recv_sem=h_rsem.at[first + at],
                device_id=who, device_id_type=MESH)
            for at, (src, dst, who) in enumerate(plan)
        ]

    def send(copies):
        for c in copies:
            c.start()

    def arrive(copies, b, buf, n, lo, hi, rc):
        for c in copies:
            c.wait()
        nothing = jnp.zeros((buf.shape[2], hi - lo), buf.dtype)

        @pl.when(row == 0)
        def _():
            buf[b, 0, :, lo:hi] = nothing
            rc[b, :, 0:8, :] = jnp.zeros((2, 8, rc.shape[3]), f32)

        @pl.when(row == nr - 1)
        def _():
            buf[b, n + 1, :, lo:hi] = nothing
            rc[b, :, n + 8 : n + 16, :] = jnp.zeros((2, 8, rc.shape[3]), f32)

        @pl.when(col == 0)
        def _():
            rc[b, 0] = jnp.zeros(rc.shape[2:], f32)

        @pl.when(col == nc - 1)
        def _():
            rc[b, 1] = jnp.zeros(rc.shape[2:], f32)

    def widen_fine(buf, b, rc):
        before, after = rc[b, 0, 7 : 7 + tall + 2, :], rc[b, 1, 7 : 7 + tall + 2, :]
        odd = buf[b, :, :, 2 * chans : 3 * chans].astype(f32)
        buf[b, :, :, 0:chans] = shifted(odd, before, 1).astype(bf16)
        even = buf[b, :, :, chans : 2 * chans].astype(f32)
        buf[b, :, :, 3 * chans : 4 * chans] = shifted(even, after, -1).astype(bf16)

    def widen_coarse(buf, b, rc):
        wide_by = rc.shape[3]
        before, after = rc[b, 0, 7 : 7 + low + 2, :], rc[b, 1, 7 : 7 + low + 2, :]
        mid = buf[b, :, :, wide_by : 2 * wide_by].astype(f32)
        buf[b, :, :, 0:wide_by] = shifted(mid, before, 1).astype(bf16)
        buf[b, :, :, 2 * wide_by : 3 * wide_by] = shifted(mid, after, -1).astype(bf16)

    def columns_fine(buf, b, sc):
        sc[b, 0] = buf[b, 1 : tall + 1, 0:16, chans : 2 * chans].astype(f32)[:, 0, :]
        sc[b, 1] = buf[b, 1 : tall + 1, half - 16 : half, 2 * chans : 3 * chans].astype(f32)[:, 15, :]

    def columns_coarse(buf, b, sc):
        wide_by = sc.shape[3]
        lanes = slice(wide_by, 2 * wide_by)
        sc[b, 0] = buf[b, 1 : low + 1, 0:16, lanes].astype(f32)[:, 0, :]
        sc[b, 1] = buf[b, 1 : low + 1, half - 16 : half, lanes].astype(f32)[:, 15, :]

    step = 8

    def split_latents(b):
        def one(k, _):
            rows = pl.ds(k * step, step)
            wide[...] = lat[b, rows].astype(f32)
            even, odd = wide[:, pl.ds(0, half, stride=2), :], wide[:, pl.ds(1, half, stride=2), :]
            V[b, pl.ds(k * step + 1, step), :, chans : 3 * chans] = jnp.concatenate([even, odd], -1).astype(bf16)
            return 0

        lax.fori_loop(0, tall // step, one, 0)

    def split_cotangent(b):
        def one(k, _):
            wide[...] = cot[b, pl.ds(k * step, step)].astype(f32)
            even, odd = wide[:, pl.ds(0, half, stride=2), :], wide[:, pl.ds(1, half, stride=2), :]
            C2[b, pl.ds(k * step, step)] = jnp.concatenate([even, odd], -1).astype(bf16)
            total = (even + odd).reshape(step // 2, 2, half, chans).sum(axis=1)
            upper = total.astype(bf16)
            rest = (total - upper.astype(f32)).astype(bf16)
            UG[b, pl.ds(k * (step // 2), step // 2)] = jnp.concatenate([upper, rest], -1)
            return 0

        lax.fori_loop(0, tall // step, one, 0)

    def prepare_forward():
        w_fwd[...] = jnp.zeros(w_fwd.shape, bf16)
        for i in range(3):
            base = i * 4 * chans
            for part in range(2):
                for j in range(3):
                    at = base + (part + j) * chans
                    w_fwd[at : at + chans, part * chans : (part + 1) * chans] = kfine[i, j]

    def prepare_back():
        w_back[...] = jnp.zeros(w_back.shape, bf16)
        for i in range(3):
            for j in range(3):
                turned = kfine[i, j].T
                for part in range(2):
                    at = i * 4 * chans + (part + 2 - j) * chans
                    w_back[at : at + chans, part * chans : (part + 1) * chans] = turned
                at = (i * 3 + 2 - j) * 2 * chans
                wc_back[at : at + 2 * chans, :] = kcoarse[i, j].T

    def prepare_lift():
        turned = lift[...].T
        upper = turned.astype(bf16)
        lift_hi[0:chans, :] = upper
        lift_hi[chans : 2 * chans, :] = upper
        lift_lo[...] = (turned - upper.astype(f32)).astype(bf16)

    flat = step * half

    def forward_fine(b):
        index = times[b]
        embedding = table[pl.ds(index, 1), :]
        embedding = jnp.concatenate([embedding, embedding], -1)

        def one(k, _):
            taps = [V[b, pl.ds(k * step + i, step)].reshape(flat, 4 * chans) for i in range(3)]
            pre = dot(jnp.concatenate(taps, -1), w_fwd[...]) + embedding
            s = sigmoid(pre)
            hidden = pre * s
            SL[b, pl.ds(k * step, step)] = (s + hidden * (1.0 - s)).reshape(step, half, 2 * chans)
            hidden = hidden.astype(bf16).astype(f32).reshape(step // 2, 2, half, 2 * chans).sum(axis=1)
            pooled = 0.25 * (hidden[:, :, :chans] + hidden[:, :, chans:])
            PO[b, pl.ds(k * (step // 2) + 1, step // 2), :, chans : 2 * chans] = pooled.astype(bf16)
            return 0

        lax.fori_loop(0, tall // step, one, 0)

    def forward_coarse(b):
        def one(k, _):
            taps = [PO[b, pl.ds(k * step + i, step)].reshape(flat, 3 * chans) for i in range(3)]
            weights = kcoarse[...].reshape(9 * chans, 2 * chans)
            pre = dot(jnp.concatenate(taps, -1), weights)
            s = sigmoid(pre)
            act = pre * s
            ACT[b, pl.ds(pl.multiple_of(k * flat, flat), flat), :] = act.astype(bf16)
            ug = UG[b, pl.ds(k * step, step)].reshape(flat, 2 * chans)
            back = dot(ug, lift_hi[...]) + dot(ug[:, :chans], lift_lo[...])
            grad = (back * (s + act * (1.0 - s))).astype(bf16)
            GC[b, pl.ds(k * step + 1, step), :, 2 * chans : 4 * chans] = grad.reshape(step, half, 2 * chans)
            return 0

        lax.fori_loop(0, low // step, one, 0)

    def backward_coarse(b):
        def one(k, total):
            taps = [GC[b, pl.ds(k * step + 2 - i, step)].reshape(flat, 6 * chans) for i in range(3)]
            pooled = 0.25 * dot(jnp.concatenate(taps, -1), wc_back[...])
            pooled = pooled.reshape(step, 1, half, chans)
            pooled = jnp.concatenate([pooled, pooled], -1)
            rows = pl.ds(k * 2 * step, 2 * step)
            direct = C2[b, rows].astype(f32).reshape(step, 2, half, 2 * chans)
            slope = SL[b, rows].reshape(step, 2, half, 2 * chans)
            grad = ((direct + pooled) * slope).astype(bf16)
            G[b, pl.ds(k * 2 * step + 1, 2 * step), :, chans : 3 * chans] = grad.reshape(2 * step, half, 2 * chans)
            return total + grad.astype(f32).reshape(2 * flat // 8, 8, 2 * chans).sum(axis=0)

        total = lax.fori_loop(0, low // step, one, jnp.zeros((8, 2 * chans), f32))
        total = total[:, :chans] + total[:, chans:]
        return total.sum(axis=0, keepdims=True)

    def backward_fine(b, part, parts):
        def one(k, _):
            taps = [G[b, pl.ds(k * step + 2 - i, step)].reshape(flat, 4 * chans) for i in range(3)]
            grad = dot(jnp.concatenate(taps, -1), w_back[...]).reshape(step, half, 2 * chans)
            rows = pl.ds(k * step, step)
            OUT[b, rows, pl.ds(0, half, stride=2), :] = grad[:, :, :chans]
            OUT[b, rows, pl.ds(1, half, stride=2), :] = grad[:, :, chans:]
            return 0

        each = tall // step // parts
        lax.fori_loop(part * each, (part + 1) * each, one, 0)
        rows = pl.ds(part * each * step, each * step)
        done = pltpu.make_async_copy(OUT.at[b, rows], grad_out.at[b, rows], out_sem.at[b * parts + part])
        done.start()
        return done

    class Reduce:
        def __init__(self, mine, first, second_in, second, owned, gathered, full, ssem, rsem, items):
            self.refs = mine, first, second_in, second, owned, gathered, full
            self.ssem, self.rsem, self.items = ssem, rsem, items
            self.share = chans // nr

        def copy(self, at, src, dst, who):
            return pltpu.make_async_remote_copy(
                src_ref=src, dst_ref=dst, send_sem=self.ssem.at[at], recv_sem=self.rsem.at[at],
                device_id=who, device_id_type=MESH)

        def rows_of(self, peer):
            return pl.ds(pl.multiple_of(peer * self.share, self.share), self.share)

        def scatter_rows(self, items):
            mine, first = self.refs[:2]
            lo, hi, group = items
            for d in range(1, nr):
                peer = lax.rem(row + d, nr)
                self.copy(group * nr + d, mine.at[pl.ds(lo, hi - lo), self.rows_of(peer)],
                          first.at[d, pl.ds(lo, hi - lo)], (peer, col)).start()

        def sum_rows(self, groups):
            mine, first, second_in = self.refs[:3]
            for lo, hi, group in groups:
                for d in range(1, nr):
                    peer = lax.rem(row + d, nr)
                    self.copy(group * nr + d, mine.at[pl.ds(lo, hi - lo), self.rows_of(peer)],
                              first.at[d, pl.ds(lo, hi - lo)], (peer, col)).wait()
            total = mine[:, self.rows_of(row), :].astype(f32)
            for d in range(1, nr):
                total = total + first[d].astype(f32)
            second_in[...] = total.astype(bf16)

        base2 = property(lambda self: 3 * nr)
        base3 = property(lambda self: 3 * nr + nc)
        base4 = property(lambda self: 3 * nr + 2 * nc)

        def scatter_cols(self):
            _, _, second_in, second = self.refs[:4]
            for d in range(1, nc):
                owner = lax.rem(col + d, nc)

                @pl.when(owner < self.items)
                def _():
                    self.copy(self.base2 + d, second_in.at[owner], second.at[d], (row, owner)).start()

        def sum_cols(self):
            _, _, second_in, second, owned = self.refs[:5]
            for d in range(1, nc):
                owner = lax.rem(col + d, nc)
                c = self.copy(self.base2 + d, second_in.at[0], second.at[d], (row, owner))
                pl.when(owner < self.items)(c.wait_send)
                pl.when(col < self.items)(c.wait_recv)

            @pl.when(col < self.items)
            def _():
                total = second_in[col].astype(f32)
                for d in range(1, nc):
                    total = total + second[d].astype(f32)
                owned[...] = total.astype(bf16)

        def gather_cols(self):
            owned, gathered = self.refs[4:6]

            @pl.when(col < self.items)
            def _():
                gathered[col] = owned[...]
                for d in range(1, nc):
                    peer = lax.rem(col + d, nc)
                    self.copy(self.base3 + d, owned, gathered.at[col], (row, peer)).start()

        def gather_rows(self):
            owned, gathered, full = self.refs[4:]
            for d in range(1, nc):
                source = lax.rem(col + nc - d, nc)
                c = self.copy(self.base3 + d, owned, gathered.at[0], (row, source))
                pl.when(col < self.items)(c.wait_send)
                pl.when(source < self.items)(c.wait_recv)
            full[:, self.rows_of(row), :] = gathered[...]
            for d in range(1, nr):
                peer = lax.rem(row + d, nr)
                self.copy(self.base4 + d, gathered, full.at[:, self.rows_of(row)], (peer, col)).start()

        def finish(self):
            gathered, full = self.refs[5:]
            for d in range(1, nr):
                peer = lax.rem(row + d, nr)
                self.copy(self.base4 + d, gathered, full.at[:, self.rows_of(row)], (peer, col)).wait()

    sum_a = Reduce(a_send, a_r1, a_s2, a_r2, a_t, a_g, a_f, a_ssem, a_rsem, 10)
    sum_b = Reduce(b_send, b_r1, b_s2, b_r2, b_t, b_g, b_f, b_ssem, b_rsem, 9)

    ex_v = [(b, V, tall, chans, 3 * chans) for b in range(count)]
    ex_p = [(b, PO, low, chans, 2 * chans) for b in range(count)]
    ex_c = [(b, GC, low, 2 * chans, 4 * chans) for b in range(count)]
    ex_g = [(b, G, tall, chans, 3 * chans) for b in range(count)]

    loads["lat0"].wait()
    split_latents(0)
    columns_fine(V, 0, sc_v)
    pl.semaphore_wait(barrier, len(partners))
    moving_v = [exchange(0, *ex_v[b], sc_v, rc_v) for b in range(count)]
    send(moving_v[0])
    loads["lat1"].wait()
    split_latents(1)
    columns_fine(V, 1, sc_v)
    send(moving_v[1])
    loads["kfine"].wait()
    prepare_forward()
    loads["table"].wait()
    loads["cot0"].wait()
    split_cotangent(0)

    moving_p = [exchange(1, *ex_p[b], sc_p, rc_p) for b in range(count)]
    for b in range(count):
        arrive(moving_v[b], *ex_v[b], rc_v)
        widen_fine(V, b, rc_v)
        forward_fine(b)
        columns_coarse(PO, b, sc_p)
        send(moving_p[b])

    loads["cot1"].wait()
    split_cotangent(1)
    loads["lift"].wait()
    prepare_lift()
    loads["kcoarse"].wait()

    moving_c = [exchange(2, *ex_c[b], sc_c, rc_c) for b in range(count)]
    for b in range(count):
        arrive(moving_p[b], *ex_p[b], rc_p)
        widen_coarse(PO, b, rc_p)
        forward_coarse(b)
        columns_coarse(GC, b, sc_c)
        send(moving_c[b])

    prepare_back()
    for b in range(count):
        PT[b] = PO[b, 1 : low + 1, :, chans : 2 * chans].reshape(low * half, chans).T
        VT[b] = V[b, 1 : tall + 1, :, chans : 3 * chans].reshape(tall * half, 2 * chans).T
    lifted = jnp.zeros((2 * chans, 2 * chans), f32)
    for b in range(count):
        lifted = lifted + dot(ACT[b].T, UG[b].reshape(low * half, 2 * chans))
    lifted = (lifted[:, :chans] + lifted[:, chans:]).astype(bf16)
    a_send[9, :, 0:chans] = lifted[:chans]
    a_send[9, :, chans : 2 * chans] = lifted[chans:]

    moving_g = [exchange(3, *ex_g[b], sc_g, rc_g) for b in range(count)]
    arrive(moving_c[0], *ex_c[0], rc_c)
    widen_coarse(GC, 0, rc_c)
    sums = [backward_coarse(0)]
    columns_fine(G, 0, sc_g)
    send(moving_g[0])
    arrive(moving_c[1], *ex_c[1], rc_c)
    widen_coarse(GC, 1, rc_c)
    sums.append(backward_coarse(1))
    columns_fine(G, 1, sc_g)
    send(moving_g[1])

    for i in range(3):
        kernel_grad = jnp.zeros((chans, 6 * chans), f32)
        for b in range(count):
            kernel_grad = kernel_grad + dot(PT[b], GC[b, 2 - i : 2 - i + low].reshape(low * half, 6 * chans))
        for j in range(3):
            at = (2 - j) * 2 * chans
            a_send[3 * i + j] = kernel_grad[:, at : at + 2 * chans].astype(bf16)
    a_groups = [(0, 10, 0)]
    sum_a.scatter_rows(a_groups[0])

    l_send[...] = jnp.concatenate(sums + [jnp.zeros((8 - count, chans), f32)], 0)
    l_moving = [
        pltpu.make_async_remote_copy(
            src_ref=l_send, dst_ref=l_r1.at[d], send_sem=l_ssem.at[d], recv_sem=l_rsem.at[d],
            device_id=(lax.rem(row + d, nr), col), device_id_type=MESH)
        for d in range(1, nr)
    ]
    send(l_moving)

    arrive(moving_g[0], *ex_g[0], rc_g)
    widen_fine(G, 0, rc_g)
    arrive(moving_g[1], *ex_g[1], rc_g)
    widen_fine(G, 1, rc_g)

    b_groups = [(3 * i, 3 * i + 3, i) for i in range(3)]
    for i in range(3):
        kernel_grad = jnp.zeros((2 * chans, 4 * chans), f32)
        for b in range(count):
            kernel_grad = kernel_grad + dot(VT[b], G[b, 2 - i : 2 - i + tall].reshape(tall * half, 4 * chans))
        for j in range(3):
            at = (2 - j) * chans
            both = kernel_grad[:chans, at : at + chans] + kernel_grad[chans:, at + chans : at + 2 * chans]
            b_send[3 * i + j] = both.astype(bf16)
        sum_b.scatter_rows(b_groups[i])
        if i == 0:
            sum_a.sum_rows(a_groups)
            sum_a.scatter_cols()
            for c in l_moving:
                c.wait()
            total = l_send[...]
            for d in range(1, nr):
                total = total + l_r1[d]
            l_s2[...] = total
            l_moving2 = [
                pltpu.make_async_remote_copy(
                    src_ref=l_s2, dst_ref=l_r2.at[d], send_sem=l_ssem.at[nr + d], recv_sem=l_rsem.at[nr + d],
                    device_id=(row, lax.rem(col + d, nc)), device_id_type=MESH)
                for d in range(1, nc)
            ]
            send(l_moving2)

    sum_a.sum_cols()
    sum_a.gather_cols()
    stores = [backward_fine(0, 0, 2)]
    sum_b.sum_rows(b_groups)
    sum_b.scatter_cols()
    sum_a.gather_rows()
    stores.append(backward_fine(0, 1, 2))
    sum_b.sum_cols()
    sum_b.gather_cols()
    stores.append(backward_fine(1, 0, 2))
    sum_b.gather_rows()
    stores.append(backward_fine(1, 1, 2))

    for c in l_moving2:
        c.wait()
    total = l_s2[...]
    for d in range(1, nc):
        total = total + l_r2[d]
    total = factor * total
    ids = lax.broadcasted_iota(jnp.int32, table_out.shape, 0)
    placed = jnp.zeros(table_out.shape, f32)
    for b in range(count):
        placed = placed + jnp.where(ids == times[b], total[b : b + 1, :], 0.0)
    table_out[...] = placed

    sum_a.finish()
    for t in range(9):
        coarse_out[t // 3, t % 3] = factor * a_f[t].astype(f32)
    lift_out[0:chans, :] = factor * a_f[9, :, 0:chans].astype(f32)
    lift_out[chans : 2 * chans, :] = factor * a_f[9, :, chans : 2 * chans].astype(f32)
    sum_b.finish()
    for t in range(9):
        fine_out[t // 3, t % 3] = factor * b_f[t].astype(f32)
    for c in stores:
        c.wait()


def solution(mesh):
    nr, nc = mesh.shape["row"], mesh.shape["col"]

    def body(latents, timesteps, time_table, conv_fine, conv_coarse, lift, cotangent):
        count, tall, broad, chans = latents.shape
        half, low = broad // 2, tall // 2
        share = chans // nr
        factor = 1.0 / math.sqrt(count * tall * broad * nr * nc)
        vm = pltpu.VMEM

        def reducer(items, wide):
            return [
                vm((items, chans, wide), bf16),
                vm((nr, items, share, wide), bf16),
                vm((items, share, wide), bf16),
                vm((nc, share, wide), bf16),
                vm((share, wide), bf16),
                vm((items, share, wide), bf16),
                vm((items, chans, wide), bf16),
            ]

        def columns(n, wide):
            return [vm((count, 2, n, wide), f32), vm((count, 2, n + 16, wide), f32)]

        scratch = [
            vm(latents.shape, bf16), vm(cotangent.shape, bf16), vm(time_table.shape, f32),
            vm(conv_fine.shape, bf16), vm(conv_coarse.shape, bf16), vm(lift.shape, f32),
            vm((8, broad, chans), f32),
            vm((12 * chans, 2 * chans), bf16), vm((12 * chans, 2 * chans), bf16), vm((18 * chans, chans), bf16),
            vm((2 * chans, 2 * chans), bf16), vm((chans, 2 * chans), bf16),
            vm((count, tall + 2, half, 4 * chans), bf16),
            vm((count, tall, half, 2 * chans), bf16),
            vm((count, tall, half, 2 * chans), f32),
            vm((count, low + 2, half, 3 * chans), bf16),
            vm((count, low, half, 2 * chans), bf16),
            vm((count, low * half, 2 * chans), bf16),
            vm((count, low + 2, half, 6 * chans), bf16),
            vm((count, tall + 2, half, 4 * chans), bf16),
            vm((count, 2 * chans, tall * half), bf16),
            vm((count, chans, low * half), bf16),
            vm(latents.shape, f32),
            *columns(tall, chans), *columns(low, chans), *columns(low, 2 * chans), *columns(tall, chans),
            *reducer(10, 2 * chans), *reducer(9, chans),
            vm((8, chans), f32), vm((nr, 8, chans), f32), vm((8, chans), f32), vm((nc, 8, chans), f32),
        ]
        dma = pltpu.SemaphoreType.DMA
        many = 4 * nr + 2 * nc
        scratch += [dma((8,)), dma((4,)), dma((64,)), dma((64,)), dma((many,)), dma((many,)),
                    dma((many,)), dma((many,)), dma((nr + nc,)), dma((nr + nc,))]
        hbm = pl.BlockSpec(memory_space=pl.ANY)
        in_vmem = pl.BlockSpec(memory_space=pltpu.VMEM)
        return pl.pallas_call(
            functools.partial(kernel, (nr, nc, factor)),
            out_shape=[
                jax.ShapeDtypeStruct(latents.shape, f32),
                jax.ShapeDtypeStruct(conv_fine.shape, f32),
                jax.ShapeDtypeStruct(conv_coarse.shape, f32),
                jax.ShapeDtypeStruct(lift.shape, f32),
                jax.ShapeDtypeStruct(time_table.shape, f32),
            ],
            in_specs=[pl.BlockSpec(memory_space=pltpu.SMEM)] + [hbm] * 6,
            out_specs=[hbm] + [in_vmem] * 4,
            scratch_shapes=scratch,
            compiler_params=pltpu.CompilerParams(
                collective_id=0, has_side_effects=True, vmem_limit_bytes=60 * 2**20),
        )(timesteps, latents, cotangent, time_table, conv_fine, conv_coarse, lift)

    in_specs = (P(None, "row", "col", None), P(), P(), P(), P(), P(), P(None, "row", "col", None))
    out_specs = (P(None, "row", "col", None), P(), P(), P(), P())
    return jax.shard_map(body, mesh=mesh, in_specs=in_specs, out_specs=out_specs, check_vma=False)
```

```python
import functools
import math

import jax
import jax.numpy as jnp
from jax import lax
from jax.experimental import pallas as pl
from jax.experimental.pallas import tpu as pltpu
from jax.sharding import PartitionSpec as P

MESH = pl.DeviceIdType.MESH
f32 = jnp.float32
bf16 = jnp.bfloat16


def dot(a, b):
    return jnp.dot(a, b, preferred_element_type=f32)


def outer(a, b):
    return lax.dot_general(a, b, (((0,), (0,)), ((), ())), preferred_element_type=f32)


def sigmoid(v):
    return 0.5 + 0.5 * jnp.tanh(0.5 * v)


def shifted(v, column, step):
    n = v.shape[1]
    ids = lax.broadcasted_iota(jnp.int32, v.shape, 1)
    edge = 0 if step == 1 else n - 1
    return jnp.where(ids == edge, column[:, None, :], pltpu.roll(v, step % n, 1))


def kernel(
    sizes,
    times, lat_in, cot_in, table_in, fine_in, coarse_in, lift_in,
    grad_out, a_out, b_out, l_out,
    lat, cot, table, kfine, kcoarse, lift,
    w_fwd, w_back, wc_back, lift_hi, lift_lo,
    V, C2, SL, PO, UG, CB, ACT, GC, G, OUT,
    sc_v, rc_v, sc_p, rc_p, sc_c, rc_c, sc_g, rc_g,
    a_theirs, a_mixed, a_send, a_r1, a_s2, a_r2, a_t, a_f,
    b_send, b_r1, b_s2, b_r2, b_t, b_f,
    l_send, l_r1, l_s2, l_r2, l_f,
    in_sem, out_sem, h_ssem, h_rsem, a_ssem, a_rsem, b_ssem, b_rsem, l_ssem, l_rsem,
):
    nr, nc = sizes
    pairs = nc // 2
    row, col = lax.axis_index("row"), lax.axis_index("col")
    core, pair = lax.rem(col, 2), col // 2
    twin = col + 1 - 2 * core
    up, down = lax.rem(row + nr - 1, nr), lax.rem(row + 1, nr)
    left, right = lax.rem(col + nc - 1, nc), lax.rem(col + 1, nc)
    other = jnp.where(core == 0, left, right)
    count, tall, half = C2.shape[0], C2.shape[1], C2.shape[2]
    low = tall // 2
    chans = lat.shape[3]

    barrier = pltpu.get_barrier_semaphore()
    partners = [(lax.rem(row + d, nr), col) for d in range(1, nr)]
    partners += [(lax.rem(row + d, nr), twin) for d in range(nr)]
    partners += [(row, lax.rem(pair + d, pairs) * 2 + core) for d in range(1, pairs)]
    partners += [(up, other), (row, other), (down, other)]
    for who in partners:
        pl.semaphore_signal(barrier, inc=1, device_id=who, device_id_type=MESH)

    loads = {}

    def load(name, src, dst):
        loads[name] = pltpu.make_async_copy(src, dst, in_sem.at[len(loads)])
        loads[name].start()

    load("lat0", lat_in.at[0], lat.at[0])
    load("lat1", lat_in.at[1], lat.at[1])
    load("kfine", fine_in, kfine)

    sending = []

    def remote(src, dst, ssem, rsem, who):
        return pltpu.make_async_remote_copy(
            src_ref=src, dst_ref=dst, send_sem=ssem, recv_sem=rsem, device_id=who, device_id_type=MESH)

    def exchange(kind, b, buf, n, lo, hi, sc, rc):
        first = (kind * count + b) * 8
        first_col, last_col = sc.at[b, 0], sc.at[b, 1]
        to_left, to_right = rc.at[b, 1], rc.at[b, 0]
        lanes = pl.ds(lo, hi - lo)
        plan = [
            (first_col.at[pl.ds(0, 8)], to_left.at[pl.ds(n + 8, 8)], (up, left)),
            (last_col.at[pl.ds(0, 8)], to_right.at[pl.ds(n + 8, 8)], (up, right)),
            (first_col.at[pl.ds(n - 8, 8)], to_left.at[pl.ds(0, 8)], (down, left)),
            (last_col.at[pl.ds(n - 8, 8)], to_right.at[pl.ds(0, 8)], (down, right)),
            (first_col, to_left.at[pl.ds(8, n)], (row, left)),
            (last_col, to_right.at[pl.ds(8, n)], (row, right)),
            (buf.at[b, 1, :, lanes], buf.at[b, n + 1, :, lanes], (up, col)),
            (buf.at[b, n, :, lanes], buf.at[b, 0, :, lanes], (down, col)),
        ]
        return [remote(src, dst, h_ssem.at[first + at], h_rsem.at[first + at], who)
                for at, (src, dst, who) in enumerate(plan)]

    def send(copies):
        for c in copies:
            c.start()
            sending.append(c)

    def arrive(copies, b, buf, n, lo, hi, rc):
        for c in copies:
            c.wait_recv()
        nothing = jnp.zeros((buf.shape[2], hi - lo), buf.dtype)

        @pl.when(row == 0)
        def _():
            buf[b, 0, :, lo:hi] = nothing
            rc[b, :, 0:8, :] = jnp.zeros((2, 8, rc.shape[3]), f32)

        @pl.when(row == nr - 1)
        def _():
            buf[b, n + 1, :, lo:hi] = nothing
            rc[b, :, n + 8 : n + 16, :] = jnp.zeros((2, 8, rc.shape[3]), f32)

        @pl.when(col == 0)
        def _():
            rc[b, 0] = jnp.zeros(rc.shape[2:], f32)

        @pl.when(col == nc - 1)
        def _():
            rc[b, 1] = jnp.zeros(rc.shape[2:], f32)

    def widen_fine(buf, b, rc):
        before, after = rc[b, 0, 7 : 7 + tall + 2, :], rc[b, 1, 7 : 7 + tall + 2, :]
        odd = buf[b, :, :, 2 * chans : 3 * chans].astype(f32)
        buf[b, :, :, 0:chans] = shifted(odd, before, 1).astype(bf16)
        even = buf[b, :, :, chans : 2 * chans].astype(f32)
        buf[b, :, :, 3 * chans : 4 * chans] = shifted(even, after, -1).astype(bf16)

    def widen_coarse(buf, b, rc):
        wide_by = rc.shape[3]
        before, after = rc[b, 0, 7 : 7 + low + 2, :], rc[b, 1, 7 : 7 + low + 2, :]
        mid = buf[b, :, :, wide_by : 2 * wide_by].astype(f32)
        buf[b, :, :, 0:wide_by] = shifted(mid, before, 1).astype(bf16)
        buf[b, :, :, 2 * wide_by : 3 * wide_by] = shifted(mid, after, -1).astype(bf16)

    def columns_fine(buf, b, sc):
        sc[b, 0] = buf[b, 1 : tall + 1, 0:16, chans : 2 * chans].astype(f32)[:, 0, :]
        sc[b, 1] = buf[b, 1 : tall + 1, half - 16 : half, 2 * chans : 3 * chans].astype(f32)[:, 15, :]

    def columns_coarse(buf, b, sc):
        wide_by = sc.shape[3]
        lanes = slice(wide_by, 2 * wide_by)
        sc[b, 0] = buf[b, 1 : low + 1, 0:16, lanes].astype(f32)[:, 0, :]
        sc[b, 1] = buf[b, 1 : low + 1, half - 16 : half, lanes].astype(f32)[:, 15, :]

    def split_latents(b):
        V[b, 1 : tall + 1, :, chans : 3 * chans] = lat[b].reshape(tall, half, 2 * chans)

    def split_cotangent(b):
        def one(k, _):
            rows = pl.ds(k * 16, 16)
            both = cot[b, rows].reshape(16, half, 2 * chans)
            C2[b, rows] = both
            total = both.astype(f32).reshape(8, 2, half, 2 * chans).sum(axis=1)
            total = total[:, :, :chans] + total[:, :, chans:]
            upper = total.astype(bf16)
            rest = (total - upper.astype(f32)).astype(bf16)
            UG[b, pl.ds(k * 8, 8)] = jnp.concatenate([upper, rest], -1)
            return 0

        lax.fori_loop(0, tall // 16, one, 0)

    def prepare_forward():
        w_fwd[...] = jnp.zeros(w_fwd.shape, bf16)
        for i in range(3):
            base = i * 4 * chans
            for part in range(2):
                for j in range(3):
                    at = base + (part + j) * chans
                    w_fwd[at : at + chans, part * chans : (part + 1) * chans] = kfine[i, j]

    def prepare_back():
        w_back[...] = jnp.zeros(w_back.shape, bf16)
        for i in range(3):
            for j in range(3):
                turned = kfine[i, j].T
                for part in range(2):
                    at = i * 4 * chans + (part + 2 - j) * chans
                    w_back[at : at + chans, part * chans : (part + 1) * chans] = turned
                at = (i * 3 + 2 - j) * 2 * chans
                wc_back[at : at + 2 * chans, :] = kcoarse[i, j].T

    def prepare_lift():
        turned = lift[...].T
        upper = turned.astype(bf16)
        lift_hi[0:chans, :] = upper
        lift_hi[chans : 2 * chans, :] = upper
        lift_lo[...] = (turned - upper.astype(f32)).astype(bf16)

    def lift_back(b):
        ug = UG[b].reshape(low * half, 2 * chans)
        CB[b] = dot(ug, lift_hi[...]) + dot(ug[:, :chans], lift_lo[...])

    def forward_fine(b):
        embedding = table[pl.ds(times[b], 1), :]
        embedding = jnp.concatenate([embedding, embedding], -1)
        step = 16

        def one(k, _):
            taps = [V[b, pl.ds(k * step + i, step)].reshape(step * half, 4 * chans) for i in range(3)]
            pre = dot(jnp.concatenate(taps, -1), w_fwd[...]) + embedding
            s = sigmoid(pre)
            hidden = pre * s
            SL[b, pl.ds(k * step, step)] = (s + hidden * (1.0 - s)).reshape(step, half, 2 * chans)
            hidden = hidden.astype(bf16).astype(f32).reshape(step // 2, 2, half, 2 * chans).sum(axis=1)
            pooled = 0.25 * (hidden[:, :, :chans] + hidden[:, :, chans:])
            PO[b, pl.ds(k * (step // 2) + 1, step // 2), :, chans : 2 * chans] = pooled.astype(bf16)
            return 0

        lax.fori_loop(0, tall // step, one, 0)

    def forward_coarse(b):
        step = 16

        def one(k, _):
            flat = step * half
            taps = [PO[b, pl.ds(k * step + i, step)].reshape(flat, 3 * chans) for i in range(3)]
            weights = kcoarse[...].reshape(9 * chans, 2 * chans)
            pre = dot(jnp.concatenate(taps, -1), weights)
            s = sigmoid(pre)
            act = pre * s
            here = pl.ds(pl.multiple_of(k * flat, flat), flat)
            ACT[b, here, :] = act.astype(bf16)
            grad = (CB[b, here, :] * (s + act * (1.0 - s))).astype(bf16)
            GC[b, pl.ds(k * step + 1, step), :, 2 * chans : 4 * chans] = grad.reshape(step, half, 2 * chans)
            return 0

        lax.fori_loop(0, low // step, one, 0)

    def backward_coarse(b):
        step = 16

        def one(k, total):
            flat = step * half
            taps = [GC[b, pl.ds(k * step + 2 - i, step)].reshape(flat, 6 * chans) for i in range(3)]
            pooled = 0.25 * dot(jnp.concatenate(taps, -1), wc_back[...])
            pooled = pooled.reshape(step, 1, half, chans)
            pooled = jnp.concatenate([pooled, pooled], -1)
            rows = pl.ds(k * 2 * step, 2 * step)
            direct = C2[b, rows].astype(f32).reshape(step, 2, half, 2 * chans)
            slope = SL[b, rows].reshape(step, 2, half, 2 * chans)
            grad = ((direct + pooled) * slope).astype(bf16)
            G[b, pl.ds(k * 2 * step + 1, 2 * step), :, chans : 3 * chans] = grad.reshape(2 * step, half, 2 * chans)
            return total + grad.astype(f32).reshape(2 * flat // 8, 8, 2 * chans).sum(axis=0)

        total = lax.fori_loop(0, low // step, one, jnp.zeros((8, 2 * chans), f32))
        total = total[:, :chans] + total[:, chans:]
        return total.sum(axis=0, keepdims=True)

    stores = []

    def backward_fine(b, part, parts):
        step = 16

        def one(k, _):
            taps = [G[b, pl.ds(k * step + 2 - i, step)].reshape(step * half, 4 * chans) for i in range(3)]
            grad = dot(jnp.concatenate(taps, -1), w_back[...]).astype(bf16)
            OUT[b, pl.ds(k * step, step)] = grad.reshape(step, 2 * half, chans)
            return 0

        each = tall // step // parts
        lax.fori_loop(part * each, (part + 1) * each, one, 0)
        rows = pl.ds(part * each * step, each * step)
        stores.append(pltpu.make_async_copy(OUT.at[b, rows], grad_out.at[b, rows], out_sem.at[len(stores)]))
        stores[-1].start()

    class Reduce:
        def __init__(self, mine, first, part, second, owned, full, ssem, rsem):
            self.refs = mine, first, part, second, owned, full
            self.ssem, self.rsem = ssem, rsem
            self.share, self.half = chans // nr, mine.shape[0] // 2
            self.base2, self.base3 = 2 * nr, 2 * nr + pairs

        def rows_of(self, peer):
            return pl.ds(pl.multiple_of(peer * self.share, self.share), self.share)

        def chunk(self, ref, owner_core, peer):
            return ref.at[pl.ds(owner_core * self.half, self.half), self.rows_of(peer)]

        def copy1(self, d, to_core):
            mine, first = self.refs[:2]
            peer, flip = lax.rem(row + d, nr), lax.rem(core + to_core, 2)
            return remote(self.chunk(mine, to_core, peer), first.at[2 * d + flip],
                          self.ssem.at[2 * d + flip], self.rsem.at[2 * d + flip], (peer, 2 * pair + to_core))

        def scatter(self, to_core):
            pl.when(core != to_core)(self.copy1(0, to_core).start)
            for d in range(1, nr):
                self.copy1(d, to_core).start()

        def copy2(self, d):
            _, _, part, second = self.refs[:4]
            return remote(part, second.at[pair], self.ssem.at[self.base2 + d], self.rsem.at[self.base2 + d],
                          (row, lax.rem(pair + d, pairs) * 2 + core))

        def cross(self):
            mine, first, part, second = self.refs[:4]
            for at in range(1, 2 * nr):
                remote(part, first.at[at], self.ssem.at[at], self.rsem.at[at], (row, twin)).wait_recv()
            total = mine[pl.ds(core * self.half, self.half), self.rows_of(row), :].astype(f32)
            for at in range(1, 2 * nr):
                total = total + first[at].astype(f32)
            part[...] = total.astype(bf16)
            second[pair] = total.astype(bf16)
            for d in range(1, pairs):
                self.copy2(d).start()

        def copy3(self, d, flip):
            owned, full = self.refs[4:]
            peer = lax.rem(row + d, nr)
            at = self.base3 + 2 * d + flip
            return remote(owned, self.chunk(full, core, row), self.ssem.at[at], self.rsem.at[at],
                          (peer, twin if flip else col))

        def collect(self):
            second, owned, full = self.refs[3:]
            for d in range(1, pairs):
                self.copy2(d).wait_recv()
            total = second[0].astype(f32)
            for at in range(1, pairs):
                total = total + second[at].astype(f32)
            owned[...] = total.astype(bf16)
            full[pl.ds(core * self.half, self.half), self.rows_of(row), :] = total.astype(bf16)

        def gather(self):
            self.collect()
            for at in range(1, 2 * nr):
                self.copy3(at // 2, at % 2).start()

        def finish(self):
            for at in range(1, 2 * nr):
                self.copy3(at // 2, at % 2).wait()
            for at in range(1, 2 * nr):
                remote(self.refs[2], self.refs[1].at[at], self.ssem.at[at], self.rsem.at[at], (row, twin)).wait_send()
            for d in range(1, pairs):
                self.copy2(d).wait_send()

    class ReduceByChip(Reduce):
        def __init__(self, theirs, mixed, *rest):
            super().__init__(*rest)
            self.theirs, self.mixed = theirs, mixed

        def copy0(self):
            give = self.refs[0].at[pl.ds((1 - core) * self.half, self.half)]
            return remote(give, self.theirs, self.ssem.at[0], self.rsem.at[0], (row, twin))

        def copy1(self, d):
            peer = lax.rem(row + d, nr)
            return remote(self.mixed.at[:, self.rows_of(peer)], self.refs[1].at[d],
                          self.ssem.at[d], self.rsem.at[d], (peer, col))

        def scatter(self):
            self.copy0().start()

        def scatter_rows(self):
            self.copy0().wait_recv()
            total = self.refs[0][pl.ds(core * self.half, self.half)].astype(f32) + self.theirs[...].astype(f32)
            self.mixed[...] = total.astype(bf16)
            for d in range(1, nr):
                self.copy1(d).start()

        def cross(self):
            _, first, part, second = self.refs[:4]
            for d in range(1, nr):
                self.copy1(d).wait_recv()
            total = self.mixed[:, self.rows_of(row), :].astype(f32)
            for d in range(1, nr):
                total = total + first[d].astype(f32)
            part[...] = total.astype(bf16)
            second[pair] = total.astype(bf16)
            for d in range(1, pairs):
                self.copy2(d).start()

        def gather(self):
            self.collect()
            for d in range(1, nr):
                self.copy3(d, 0).start()

        def copy4(self):
            done = self.refs[5].at[pl.ds(core * self.half, self.half)]
            return remote(done, done, self.ssem.at[nr], self.rsem.at[nr], (row, twin))

        def gather_cores(self):
            for d in range(1, nr):
                self.copy3(d, 0).wait_recv()
            self.copy4().start()

        def finish(self):
            self.copy4().wait()
            self.copy0().wait_send()
            for d in range(1, nr):
                self.copy1(d).wait_send()
                self.copy3(d, 0).wait_send()
            for d in range(1, pairs):
                self.copy2(d).wait_send()

    sum_a = ReduceByChip(a_theirs, a_mixed, a_send, a_r1, a_s2, a_r2, a_t, a_f, a_ssem, a_rsem)
    sum_b = Reduce(b_send, b_r1, b_s2, b_r2, b_t, b_f, b_ssem, b_rsem)

    ex_v = [(b, V, tall, chans, 3 * chans) for b in range(count)]
    ex_p = [(b, PO, low, chans, 2 * chans) for b in range(count)]
    ex_c = [(b, GC, low, 2 * chans, 4 * chans) for b in range(count)]
    ex_g = [(b, G, tall, chans, 3 * chans) for b in range(count)]
    loads["lat0"].wait()
    split_latents(0)
    columns_fine(V, 0, sc_v)
    pl.semaphore_wait(barrier, len(partners))
    moving_v = [exchange(0, *ex_v[b], sc_v, rc_v) for b in range(count)]
    send(moving_v[0])
    loads["lat1"].wait()
    split_latents(1)
    columns_fine(V, 1, sc_v)
    send(moving_v[1])
    load("table", table_in, table)
    load("cot0", cot_in.at[0], cot.at[0])
    load("cot1", cot_in.at[1], cot.at[1])
    load("lift", lift_in, lift)
    load("kcoarse", coarse_in, kcoarse)
    loads["kfine"].wait()
    prepare_forward()
    loads["cot0"].wait()
    split_cotangent(0)
    loads["cot1"].wait()
    split_cotangent(1)
    loads["table"].wait()
    loads["kcoarse"].wait()

    moving_p = [exchange(1, *ex_p[b], sc_p, rc_p) for b in range(count)]
    for b in range(count):
        arrive(moving_v[b], *ex_v[b], rc_v)
        widen_fine(V, b, rc_v)
        forward_fine(b)
        columns_coarse(PO, b, sc_p)
        send(moving_p[b])

    loads["lift"].wait()
    prepare_lift()
    lift_back(0)
    lift_back(1)
    prepare_back()

    moving_c = [exchange(2, *ex_c[b], sc_c, rc_c) for b in range(count)]
    for b in range(count):
        arrive(moving_p[b], *ex_p[b], rc_p)
        widen_coarse(PO, b, rc_p)
        forward_coarse(b)
        columns_coarse(GC, b, sc_c)
        send(moving_c[b])

    lifted = jnp.zeros((2 * chans, 2 * chans), f32)
    for b in range(count):
        lifted = lifted + outer(ACT[b], UG[b].reshape(low * half, 2 * chans))
    lifted = (lifted[:, :chans] + lifted[:, chans:]).astype(bf16)
    a_send[9, :, 0:chans] = lifted[:chans]
    a_send[9, :, chans : 2 * chans] = lifted[chans:]
    for i in range(3):
        kernel_grad = jnp.zeros((2 * chans, 3 * chans), f32)
        for b in range(count):
            grad = GC[b, 1 : low + 1, :, 2 * chans : 4 * chans].reshape(low * half, 2 * chans)
            kernel_grad = kernel_grad + outer(grad, PO[b, i : i + low].reshape(low * half, 3 * chans))
        for j in range(3):
            a_send[3 * i + j] = kernel_grad[:, j * chans : (j + 1) * chans].T.astype(bf16)
    sum_a.scatter()

    moving_g = [exchange(3, *ex_g[b], sc_g, rc_g) for b in range(count)]
    sums = []
    for b in range(count):
        arrive(moving_c[b], *ex_c[b], rc_c)
        widen_coarse(GC, b, rc_c)
        sums.append(backward_coarse(b))
        columns_fine(G, b, sc_g)
        send(moving_g[b])
        if b == 0:
            sum_a.scatter_rows()

    l_send[...] = jnp.concatenate(sums + [jnp.zeros((8 - count, chans), f32)], 0)
    l_moving = [
        remote(l_send, l_r1.at[2 * row + core], l_ssem.at[at], l_rsem.at[at],
               (lax.rem(row + at // 2, nr), twin if at % 2 else col))
        for at in range(1, 2 * nr)
    ]
    send(l_moving)
    l_r1[2 * row + core] = l_send[...]

    for i in range(3):
        kernel_grad = jnp.zeros((2 * chans, 4 * chans), f32)
        for b in range(count):
            grad = G[b, 1 : tall + 1, :, chans : 3 * chans].reshape(tall * half, 2 * chans)
            kernel_grad = kernel_grad + outer(grad, V[b, i : i + tall].reshape(tall * half, 4 * chans))
        for j in range(3):
            both = kernel_grad[:chans, j * chans : (j + 1) * chans]
            both = both + kernel_grad[chans:, (j + 1) * chans : (j + 2) * chans]
            b_send[3 * i + j] = both.astype(bf16)
        if i == 1:
            sum_b.scatter(0)
    b_send[9] = jnp.zeros(b_send.shape[1:], bf16)
    sum_b.scatter(1)

    arrive(moving_g[0], *ex_g[0], rc_g)
    widen_fine(G, 0, rc_g)
    sum_a.cross()
    backward_fine(0, 0, 2)
    backward_fine(0, 1, 2)
    for c in l_moving:
        c.wait_recv()
    total = l_r1[0]
    for at in range(1, 2 * nr):
        total = total + l_r1[at]
    l_s2[...] = total
    l_r2[pair] = total
    l_moving2 = [
        remote(l_s2, l_r2.at[pair], l_ssem.at[2 * nr + d], l_rsem.at[2 * nr + d],
               (row, lax.rem(pair + d, pairs) * 2 + core))
        for d in range(1, pairs)
    ]
    send(l_moving2)

    arrive(moving_g[1], *ex_g[1], rc_g)
    widen_fine(G, 1, rc_g)
    backward_fine(1, 0, 2)
    sum_b.cross()
    backward_fine(1, 1, 2)
    sum_a.gather()
    sum_b.gather()
    sum_a.gather_cores()

    for c in l_moving2:
        c.wait_recv()
    total = l_r2[0]
    for d in range(1, pairs):
        total = total + l_r2[d]
    l_send_done = pltpu.make_async_copy(l_f, l_out, out_sem.at[len(stores)])
    l_f[...] = total
    l_send_done.start()
    stores.append(l_send_done)
    sum_a.finish()
    stores.append(pltpu.make_async_copy(a_f, a_out, out_sem.at[len(stores)]))
    stores[-1].start()
    for c in sending:
        c.wait_send()
    sum_b.finish()
    stores.append(pltpu.make_async_copy(b_f, b_out, out_sem.at[len(stores)]))
    stores[-1].start()
    for c in stores:
        c.wait()


def finishing(
    factor, parts, times, grad_in, a_in, b_in, l_in, grad_out, fine_out, coarse_out, lift_out, table_out,
    g16, a16, b16, l32, g32, fine, coarse, lift, table, in_sem, out_sem,
):
    count, tall, chans = g16.shape[0], g16.shape[1], g16.shape[3]
    each = tall // parts
    pieces = [(b, pl.ds(p * each, each)) for b in range(count) for p in range(parts)]
    loads = [pltpu.make_async_copy(grad_in.at[b, rows], g16.at[b, rows], in_sem.at[3 + at])
             for at, (b, rows) in enumerate(pieces)]
    loads += [pltpu.make_async_copy(l_in, l32, in_sem.at[0]), pltpu.make_async_copy(b_in, b16, in_sem.at[1]),
              pltpu.make_async_copy(a_in, a16, in_sem.at[2])]
    for c in loads:
        c.start()
    stores = []

    def store(src, dst):
        stores.append(pltpu.make_async_copy(src, dst, out_sem.at[len(stores)]))
        stores[-1].start()

    for at, (b, rows) in enumerate(pieces):
        loads[at].wait()
        g32[b, rows] = g16[b, rows].astype(f32)
        store(g32.at[b, rows], grad_out.at[b, rows])
    loads[-3].wait()
    total = factor * l32[...]
    ids = lax.broadcasted_iota(jnp.int32, table.shape, 0)
    placed = jnp.zeros(table.shape, f32)
    for b in range(count):
        placed = placed + jnp.where(ids == times[b], total[b : b + 1, :], 0.0)
    table[...] = placed
    store(table, table_out)
    loads[-2].wait()
    for t in range(9):
        fine[t // 3, t % 3] = factor * b16[t].astype(f32).T
    store(fine, fine_out)
    loads[-1].wait()
    for t in range(9):
        coarse[t // 3, t % 3] = factor * a16[t].astype(f32)
    store(coarse, coarse_out)
    lift[0:chans, :] = factor * a16[9, :, 0:chans].astype(f32)
    lift[chans : 2 * chans, :] = factor * a16[9, :, chans : 2 * chans].astype(f32)
    store(lift, lift_out)
    for c in stores:
        c.wait()


def solution(mesh):
    nr, nc = mesh.shape["row"], mesh.shape["col"]

    def body(latents, timesteps, time_table, conv_fine, conv_coarse, lift, cotangent):
        count, tall, broad, chans = latents.shape
        half, low = broad // 2, tall // 2
        share, pairs = chans // nr, nc // 2
        factor = 1.0 / math.sqrt(count * tall * broad * nr * nc)
        vm = pltpu.VMEM
        dma = pltpu.SemaphoreType.DMA
        hbm = pl.BlockSpec(memory_space=pl.ANY)
        smem = pl.BlockSpec(memory_space=pltpu.SMEM)

        def reducer(wide, peers):
            return [
                vm((10, chans, wide), bf16),
                vm((peers, 5, share, wide), bf16),
                vm((5, share, wide), bf16),
                vm((pairs, 5, share, wide), bf16),
                vm((5, share, wide), bf16),
                vm((10, chans, wide), bf16),
            ]

        def columns(n, wide):
            return [vm((count, 2, n, wide), f32), vm((count, 2, n + 16, wide), f32)]

        scratch = [
            vm(latents.shape, bf16), vm(cotangent.shape, bf16), vm(time_table.shape, f32),
            vm(conv_fine.shape, bf16), vm(conv_coarse.shape, bf16), vm(lift.shape, f32),
            vm((12 * chans, 2 * chans), bf16), vm((12 * chans, 2 * chans), bf16), vm((18 * chans, chans), bf16),
            vm((2 * chans, 2 * chans), bf16), vm((chans, 2 * chans), bf16),
            vm((count, tall + 2, half, 4 * chans), bf16),
            vm((count, tall, half, 2 * chans), bf16),
            vm((count, tall, half, 2 * chans), f32),
            vm((count, low + 2, half, 3 * chans), bf16),
            vm((count, low, half, 2 * chans), bf16),
            vm((count, low * half, 2 * chans), f32),
            vm((count, low * half, 2 * chans), bf16),
            vm((count, low + 2, half, 6 * chans), bf16),
            vm((count, tall + 2, half, 4 * chans), bf16),
            vm(latents.shape, bf16),
            *columns(tall, chans), *columns(low, chans), *columns(low, 2 * chans), *columns(tall, chans),
            vm((5, chans, 2 * chans), bf16), vm((5, chans, 2 * chans), bf16), *reducer(2 * chans, nr), *reducer(chans, 2 * nr),
            vm((8, chans), f32), vm((2 * nr, 8, chans), f32), vm((8, chans), f32), vm((pairs, 8, chans), f32),
            vm((8, chans), f32),
        ]
        many = 4 * nr + pairs
        scratch += [dma((8,)), dma((8,)), dma((64,)), dma((64,)), dma((many,)), dma((many,)),
                    dma((many,)), dma((many,)), dma((2 * nr + pairs,)), dma((2 * nr + pairs,))]
        shape = jax.ShapeDtypeStruct
        grad, sum_a, sum_b, sum_l = pl.pallas_call(
            functools.partial(kernel, (nr, nc)),
            out_shape=[shape(latents.shape, bf16), shape((10, chans, 2 * chans), bf16),
                       shape((10, chans, chans), bf16), shape((8, chans), f32)],
            in_specs=[smem] + [hbm] * 6,
            out_specs=[hbm] * 4,
            scratch_shapes=scratch,
            compiler_params=pltpu.CompilerParams(
                collective_id=0, has_side_effects=True, vmem_limit_bytes=60 * 2**20),
        )(timesteps, latents, cotangent, time_table, conv_fine, conv_coarse, lift)

        parts = 4
        results = [latents.shape, conv_fine.shape, conv_coarse.shape, lift.shape, time_table.shape]
        return pl.pallas_call(
            functools.partial(finishing, factor, parts),
            out_shape=[shape(s, f32) for s in results],
            in_specs=[smem] + [hbm] * 4,
            out_specs=[hbm] * 5,
            scratch_shapes=[
                vm(latents.shape, bf16), vm(sum_a.shape, bf16), vm(sum_b.shape, bf16), vm(sum_l.shape, f32),
                *[vm(s, f32) for s in results], dma((3 + count * parts,)), dma((4 + count * parts,))],
            compiler_params=pltpu.CompilerParams(vmem_limit_bytes=60 * 2**20),
        )(timesteps, grad, sum_a, sum_b, sum_l)

    in_specs = (P(None, "row", "col", None), P(), P(), P(), P(), P(), P(None, "row", "col", None))
    out_specs = (P(None, "row", "col", None), P(), P(), P(), P())
    return jax.shard_map(body, mesh=mesh, in_specs=in_specs, out_specs=out_specs, check_vma=False)
```

```python
import functools
import math

import jax
import jax.numpy as jnp
from jax import lax
from jax.experimental import pallas as pl
from jax.experimental.pallas import tpu as pltpu
from jax.sharding import PartitionSpec as P

MESH = pl.DeviceIdType.MESH
f32 = jnp.float32
bf16 = jnp.bfloat16


def dot(a, b):
    return jnp.dot(a, b, preferred_element_type=f32)


def outer(a, b):
    return lax.dot_general(a, b, (((0,), (0,)), ((), ())), preferred_element_type=f32)


def sigmoid(v):
    return 0.5 + 0.5 * jnp.tanh(0.5 * v)


def shifted(v, column, step):
    n = v.shape[1]
    ids = lax.broadcasted_iota(jnp.int32, v.shape, 1)
    edge = 0 if step == 1 else n - 1
    return jnp.where(ids == edge, column[:, None, :], pltpu.roll(v, step % n, 1))


def kernel(
    sizes,
    times_in, lat_in, cot_in, table_in, fine_in, coarse_in, lift_in,
    grad_out, a_out, b_out, l_out,
    times, lat, cot, table, kfine, kcoarse, lift,
    w_fwd, w_back, wc_back, lift_hi, lift_lo,
    V, C2, SL, PO, UG, CB, ACT, GC, G, OUT,
    sc_v, rc_v, sc_p, rc_p, sc_c, rc_c, sc_g, rc_g,
    a_theirs, a_mixed, a_send, a_r1, a_s2, a_r2, a_t, a_f,
    b_send, b_r1, b_s2, b_r2, b_t, b_f,
    l_send, l_r1, l_s2, l_r2, l_f,
    in_sem, out_sem, h_ssem, h_rsem, a_ssem, a_rsem, b_ssem, b_rsem, l_ssem, l_rsem,
):
    nr, nc = sizes
    pairs = nc // 2
    row, col = lax.axis_index("row"), lax.axis_index("col")
    core, pair = lax.rem(col, 2), col // 2
    twin = col + 1 - 2 * core
    up, down = lax.rem(row + nr - 1, nr), lax.rem(row + 1, nr)
    left, right = lax.rem(col + nc - 1, nc), lax.rem(col + 1, nc)
    other = jnp.where(core == 0, left, right)
    count, tall, half = C2.shape[0], C2.shape[1], C2.shape[2]
    low = tall // 2
    chans = lat.shape[3]

    barrier = pltpu.get_barrier_semaphore()
    partners = [(lax.rem(row + d, nr), col) for d in range(1, nr)]
    partners += [(lax.rem(row + d, nr), twin) for d in range(nr)]
    partners += [(row, lax.rem(pair + d, pairs) * 2 + core) for d in range(1, pairs)]
    partners += [(up, other), (row, other), (down, other)]
    for who in partners:
        pl.semaphore_signal(barrier, inc=1, device_id=who, device_id_type=MESH)

    loads = {}

    def load(name, src, dst):
        loads[name] = pltpu.make_async_copy(src, dst, in_sem.at[len(loads)])
        loads[name].start()

    load("lat0", lat_in.at[0], lat.at[0])
    load("lat1", lat_in.at[1], lat.at[1])
    load("kfine", fine_in, kfine)
    load("times", times_in, times)

    sending = []

    def remote(src, dst, ssem, rsem, who):
        return pltpu.make_async_remote_copy(
            src_ref=src, dst_ref=dst, send_sem=ssem, recv_sem=rsem, device_id=who, device_id_type=MESH)

    def exchange(kind, b, buf, n, lo, hi, sc, rc):
        at = kind * count + b
        first_col, last_col = sc.at[b, 0], sc.at[b, 1]
        to_left, to_right = rc.at[b, 1], rc.at[b, 0]
        lanes = pl.ds(lo, hi - lo)
        plan = [
            (first_col.at[pl.ds(0, 8)], to_left.at[pl.ds(n + 8, 8)], (up, left)),
            (last_col.at[pl.ds(0, 8)], to_right.at[pl.ds(n + 8, 8)], (up, right)),
            (first_col.at[pl.ds(n - 8, 8)], to_left.at[pl.ds(0, 8)], (down, left)),
            (last_col.at[pl.ds(n - 8, 8)], to_right.at[pl.ds(0, 8)], (down, right)),
            (first_col, to_left.at[pl.ds(8, n)], (row, left)),
            (last_col, to_right.at[pl.ds(8, n)], (row, right)),
            (buf.at[b, 1, :, lanes], buf.at[b, n + 1, :, lanes], (up, col)),
            (buf.at[b, n, :, lanes], buf.at[b, 0, :, lanes], (down, col)),
        ]
        rows = sum(math.prod(src.shape) * jnp.dtype(src.dtype).itemsize for src, _, _ in plan) // (4 * chans)
        every = table.at[pl.ds(0, rows)]
        return ([remote(src, dst, h_ssem.at[at], h_rsem.at[at], who) for src, dst, who in plan],
                remote(every, every, h_ssem.at[at], h_rsem.at[at], (row, twin)))

    def send(copies):
        for c in copies[0]:
            c.start()
        sending.append(copies[1])

    def arrive(copies, b, buf, n, lo, hi, rc):
        copies[1].wait_recv()
        nothing = jnp.zeros((buf.shape[2], hi - lo), buf.dtype)

        @pl.when(row == 0)
        def _():
            buf[b, 0, :, lo:hi] = nothing
            rc[b, :, 0:8, :] = jnp.zeros((2, 8, rc.shape[3]), f32)

        @pl.when(row == nr - 1)
        def _():
            buf[b, n + 1, :, lo:hi] = nothing
            rc[b, :, n + 8 : n + 16, :] = jnp.zeros((2, 8, rc.shape[3]), f32)

        @pl.when(col == 0)
        def _():
            rc[b, 0] = jnp.zeros(rc.shape[2:], f32)

        @pl.when(col == nc - 1)
        def _():
            rc[b, 1] = jnp.zeros(rc.shape[2:], f32)

    def widen_fine(buf, b, rc):
        before, after = rc[b, 0, 7 : 7 + tall + 2, :], rc[b, 1, 7 : 7 + tall + 2, :]
        odd = buf[b, :, :, 2 * chans : 3 * chans].astype(f32)
        buf[b, :, :, 0:chans] = shifted(odd, before, 1).astype(bf16)
        even = buf[b, :, :, chans : 2 * chans].astype(f32)
        buf[b, :, :, 3 * chans : 4 * chans] = shifted(even, after, -1).astype(bf16)

    def widen_coarse(buf, b, rc):
        wide_by = rc.shape[3]
        before, after = rc[b, 0, 7 : 7 + low + 2, :], rc[b, 1, 7 : 7 + low + 2, :]
        mid = buf[b, :, :, wide_by : 2 * wide_by].astype(f32)
        buf[b, :, :, 0:wide_by] = shifted(mid, before, 1).astype(bf16)
        buf[b, :, :, 2 * wide_by : 3 * wide_by] = shifted(mid, after, -1).astype(bf16)

    def columns_fine(buf, b, sc):
        sc[b, 0] = buf[b, 1 : tall + 1, 0:16, chans : 2 * chans].astype(f32)[:, 0, :]
        sc[b, 1] = buf[b, 1 : tall + 1, half - 16 : half, 2 * chans : 3 * chans].astype(f32)[:, 15, :]

    def columns_coarse(buf, b, sc):
        wide_by = sc.shape[3]
        lanes = slice(wide_by, 2 * wide_by)
        sc[b, 0] = buf[b, 1 : low + 1, 0:16, lanes].astype(f32)[:, 0, :]
        sc[b, 1] = buf[b, 1 : low + 1, half - 16 : half, lanes].astype(f32)[:, 15, :]

    def split_latents(b):
        V[b, 1 : tall + 1, :, chans : 3 * chans] = lat[b].reshape(tall, half, 2 * chans)

    def split_cotangent(b):
        def one(k, _):
            rows = pl.ds(k * 16, 16)
            both = cot[b, rows].reshape(16, half, 2 * chans)
            C2[b, rows] = both
            total = both.astype(f32).reshape(8, 2, half, 2 * chans).sum(axis=1)
            total = total[:, :, :chans] + total[:, :, chans:]
            upper = total.astype(bf16)
            rest = (total - upper.astype(f32)).astype(bf16)
            UG[b, pl.ds(k * 8, 8)] = jnp.concatenate([upper, rest], -1)
            return 0

        lax.fori_loop(0, tall // 16, one, 0)

    def prepare_forward():
        w_fwd[...] = jnp.zeros(w_fwd.shape, bf16)
        for i in range(3):
            base = i * 4 * chans
            for part in range(2):
                for j in range(3):
                    at = base + (part + j) * chans
                    w_fwd[at : at + chans, part * chans : (part + 1) * chans] = kfine[i, j]

    def prepare_back():
        w_back[...] = jnp.zeros(w_back.shape, bf16)
        for i in range(3):
            for j in range(3):
                turned = kfine[i, j].T
                for part in range(2):
                    at = i * 4 * chans + (part + 2 - j) * chans
                    w_back[at : at + chans, part * chans : (part + 1) * chans] = turned
                at = (i * 3 + 2 - j) * 2 * chans
                wc_back[at : at + 2 * chans, :] = kcoarse[i, j].T

    def prepare_lift():
        turned = lift[...].T
        upper = turned.astype(bf16)
        lift_hi[0:chans, :] = upper
        lift_hi[chans : 2 * chans, :] = upper
        lift_lo[...] = (turned - upper.astype(f32)).astype(bf16)

    def lift_back(b):
        ug = UG[b].reshape(low * half, 2 * chans)
        CB[b] = dot(ug, lift_hi[...]) + dot(ug[:, :chans], lift_lo[...])

    def forward_fine(b):
        embedding = table[pl.ds(times[b], 1), :]
        embedding = jnp.concatenate([embedding, embedding], -1)
        step = 32

        def one(k, _):
            taps = [V[b, pl.ds(k * step + i, step)].reshape(step * half, 4 * chans) for i in range(3)]
            pre = dot(jnp.concatenate(taps, -1), w_fwd[...]) + embedding
            s = sigmoid(pre)
            hidden = pre * s
            SL[b, pl.ds(k * step, step)] = (s + hidden * (1.0 - s)).reshape(step, half, 2 * chans)
            hidden = hidden.astype(bf16).astype(f32).reshape(step // 2, 2, half, 2 * chans).sum(axis=1)
            pooled = 0.25 * (hidden[:, :, :chans] + hidden[:, :, chans:])
            PO[b, pl.ds(k * (step // 2) + 1, step // 2), :, chans : 2 * chans] = pooled.astype(bf16)
            return 0

        lax.fori_loop(0, tall // step, one, 0)

    def forward_coarse(b):
        step = 32

        def one(k, _):
            flat = step * half
            taps = [PO[b, pl.ds(k * step + i, step)].reshape(flat, 3 * chans) for i in range(3)]
            weights = kcoarse[...].reshape(9 * chans, 2 * chans)
            pre = dot(jnp.concatenate(taps, -1), weights)
            s = sigmoid(pre)
            act = pre * s
            here = pl.ds(pl.multiple_of(k * flat, flat), flat)
            ACT[b, here, :] = act.astype(bf16)
            grad = (CB[b, here, :] * (s + act * (1.0 - s))).astype(bf16)
            GC[b, pl.ds(k * step + 1, step), :, 2 * chans : 4 * chans] = grad.reshape(step, half, 2 * chans)
            return 0

        lax.fori_loop(0, low // step, one, 0)

    def backward_coarse(b):
        step = 32

        def one(k, total):
            flat = step * half
            taps = [GC[b, pl.ds(k * step + 2 - i, step)].reshape(flat, 6 * chans) for i in range(3)]
            pooled = 0.25 * dot(jnp.concatenate(taps, -1), wc_back[...])
            pooled = pooled.reshape(step, 1, half, chans)
            pooled = jnp.concatenate([pooled, pooled], -1)
            rows = pl.ds(k * 2 * step, 2 * step)
            direct = C2[b, rows].astype(f32).reshape(step, 2, half, 2 * chans)
            slope = SL[b, rows].reshape(step, 2, half, 2 * chans)
            grad = ((direct + pooled) * slope).astype(bf16)
            G[b, pl.ds(k * 2 * step + 1, 2 * step), :, chans : 3 * chans] = grad.reshape(2 * step, half, 2 * chans)
            return total + grad.astype(f32).reshape(2 * flat // 8, 8, 2 * chans).sum(axis=0)

        total = lax.fori_loop(0, low // step, one, jnp.zeros((8, 2 * chans), f32))
        total = total[:, :chans] + total[:, chans:]
        return total.sum(axis=0, keepdims=True)

    stores = []

    def backward_fine(b, part, parts):
        step = 32

        def one(k, _):
            taps = [G[b, pl.ds(k * step + 2 - i, step)].reshape(step * half, 4 * chans) for i in range(3)]
            grad = dot(jnp.concatenate(taps, -1), w_back[...]).astype(bf16)
            OUT[b, pl.ds(k * step, step)] = grad.reshape(step, 2 * half, chans)
            return 0

        each = tall // step // parts
        lax.fori_loop(part * each, (part + 1) * each, one, 0)
        rows = pl.ds(part * each * step, each * step)
        stores.append(pltpu.make_async_copy(OUT.at[b, rows], grad_out.at[b, rows], out_sem.at[len(stores)]))
        stores[-1].start()

    class Reduce:
        def __init__(self, mine, first, part, second, owned, full, ssem, rsem):
            self.refs = mine, first, part, second, owned, full
            self.ssem, self.rsem = ssem, rsem
            self.share, self.half = chans // nr, mine.shape[0] // 2
            self.peers = first.shape[0] - 1

        def all_of(self, phase):
            every = self.refs[3].at[pl.ds(0, pairs - 1)] if phase == 2 else self.refs[1].at[pl.ds(1, self.peers)]
            return remote(every, every, self.ssem.at[phase], self.rsem.at[phase], (row, twin))

        def rows_of(self, peer):
            return pl.ds(pl.multiple_of(peer * self.share, self.share), self.share)

        def chunk(self, ref, owner_core, peer):
            return ref.at[pl.ds(owner_core * self.half, self.half), self.rows_of(peer)]

        def copy1(self, d, to_core):
            mine, first = self.refs[:2]
            peer, flip = lax.rem(row + d, nr), lax.rem(core + to_core, 2)
            return remote(self.chunk(mine, to_core, peer), first.at[2 * d + flip],
                          self.ssem.at[1], self.rsem.at[1], (peer, 2 * pair + to_core))

        def scatter(self, to_core):
            pl.when(core != to_core)(self.copy1(0, to_core).start)
            for d in range(1, nr):
                self.copy1(d, to_core).start()

        def copy2(self, d):
            _, _, part, second = self.refs[:4]
            return remote(part, second.at[pair], self.ssem.at[2], self.rsem.at[2],
                          (row, lax.rem(pair + d, pairs) * 2 + core))

        def cross(self):
            mine, first, part, second = self.refs[:4]
            self.all_of(1).wait_recv()
            total = mine[pl.ds(core * self.half, self.half), self.rows_of(row), :].astype(f32)
            for at in range(1, 2 * nr):
                total = total + first[at].astype(f32)
            part[...] = total.astype(bf16)
            second[pair] = total.astype(bf16)
            for d in range(1, pairs):
                self.copy2(d).start()

        def copy3(self, d, flip):
            owned, full = self.refs[4:]
            peer = lax.rem(row + d, nr)
            return remote(owned, self.chunk(full, core, row), self.ssem.at[3], self.rsem.at[3],
                          (peer, twin if flip else col))

        def collect(self):
            second, owned, full = self.refs[3:]
            self.all_of(2).wait_recv()
            total = second[0].astype(f32)
            for at in range(1, pairs):
                total = total + second[at].astype(f32)
            owned[...] = total.astype(bf16)
            full[pl.ds(core * self.half, self.half), self.rows_of(row), :] = total.astype(bf16)

        def gather(self):
            self.collect()
            for at in range(1, 2 * nr):
                self.copy3(at // 2, at % 2).start()

        def finish(self):
            self.all_of(3).wait_recv()
            for phase in range(1, 4):
                self.all_of(phase).wait_send()

    class ReduceByChip(Reduce):
        def __init__(self, theirs, mixed, *rest):
            super().__init__(*rest)
            self.theirs, self.mixed = theirs, mixed

        def copy0(self):
            give = self.refs[0].at[pl.ds((1 - core) * self.half, self.half)]
            return remote(give, self.theirs, self.ssem.at[0], self.rsem.at[0], (row, twin))

        def copy1(self, d):
            peer = lax.rem(row + d, nr)
            return remote(self.mixed.at[:, self.rows_of(peer)], self.refs[1].at[d],
                          self.ssem.at[1], self.rsem.at[1], (peer, col))

        def scatter(self):
            self.copy0().start()

        def scatter_rows(self):
            self.copy0().wait_recv()
            total = self.refs[0][pl.ds(core * self.half, self.half)] + self.theirs[...]
            self.mixed[...] = total.astype(bf16)
            for d in range(1, nr):
                self.copy1(d).start()

        def cross(self):
            _, first, part, second = self.refs[:4]
            self.all_of(1).wait_recv()
            total = self.mixed[:, self.rows_of(row), :].astype(f32)
            for d in range(1, nr):
                total = total + first[d].astype(f32)
            part[...] = total.astype(bf16)
            second[pair] = total.astype(bf16)
            for d in range(1, pairs):
                self.copy2(d).start()

        def gather(self):
            self.collect()
            for d in range(1, nr):
                self.copy3(d, 0).start()

        def copy4(self):
            done = self.refs[5].at[pl.ds(core * self.half, self.half)]
            return remote(done, done, self.ssem.at[4], self.rsem.at[4], (row, twin))

        def gather_cores(self):
            self.all_of(3).wait_recv()
            self.copy4().start()

        def finish(self):
            self.copy4().wait()
            self.copy0().wait_send()
            for phase in range(1, 4):
                self.all_of(phase).wait_send()

    sum_a = ReduceByChip(a_theirs, a_mixed, a_send, a_r1, a_s2, a_r2, a_t, a_f, a_ssem, a_rsem)
    sum_b = Reduce(b_send, b_r1, b_s2, b_r2, b_t, b_f, b_ssem, b_rsem)

    ex_v = [(b, V, tall, chans, 3 * chans) for b in range(count)]
    ex_p = [(b, PO, low, chans, 2 * chans) for b in range(count)]
    ex_c = [(b, GC, low, 2 * chans, 4 * chans) for b in range(count)]
    ex_g = [(b, G, tall, chans, 3 * chans) for b in range(count)]
    loads["lat0"].wait()
    split_latents(0)
    columns_fine(V, 0, sc_v)
    pl.semaphore_wait(barrier, len(partners))
    moving_v = [exchange(0, *ex_v[b], sc_v, rc_v) for b in range(count)]
    send(moving_v[0])
    loads["lat1"].wait()
    split_latents(1)
    columns_fine(V, 1, sc_v)
    send(moving_v[1])
    load("table", table_in, table)
    load("cot0", cot_in.at[0], cot.at[0])
    load("cot1", cot_in.at[1], cot.at[1])
    load("lift", lift_in, lift)
    load("kcoarse", coarse_in, kcoarse)
    loads["kfine"].wait()
    prepare_forward()
    loads["cot0"].wait()
    split_cotangent(0)
    loads["cot1"].wait()
    split_cotangent(1)
    loads["table"].wait()
    loads["times"].wait()
    loads["kcoarse"].wait()

    moving_p = [exchange(1, *ex_p[b], sc_p, rc_p) for b in range(count)]
    for b in range(count):
        arrive(moving_v[b], *ex_v[b], rc_v)
        widen_fine(V, b, rc_v)
        forward_fine(b)
        columns_coarse(PO, b, sc_p)
        send(moving_p[b])

    loads["lift"].wait()
    prepare_lift()
    lift_back(0)
    lift_back(1)
    prepare_back()

    moving_c = [exchange(2, *ex_c[b], sc_c, rc_c) for b in range(count)]
    for b in range(count):
        arrive(moving_p[b], *ex_p[b], rc_p)
        widen_coarse(PO, b, rc_p)
        forward_coarse(b)
        columns_coarse(GC, b, sc_c)
        send(moving_c[b])

    lifted = jnp.zeros((2 * chans, 2 * chans), f32)
    for b in range(count):
        lifted = lifted + outer(ACT[b], UG[b].reshape(low * half, 2 * chans))
    lifted = lifted[:, :chans] + lifted[:, chans:]
    a_send[9, :, 0:chans] = lifted[:chans]
    a_send[9, :, chans : 2 * chans] = lifted[chans:]
    for i in range(3):
        kernel_grad = jnp.zeros((2 * chans, 3 * chans), f32)
        for b in range(count):
            grad = GC[b, 1 : low + 1, :, 2 * chans : 4 * chans].reshape(low * half, 2 * chans)
            kernel_grad = kernel_grad + outer(grad, PO[b, i : i + low].reshape(low * half, 3 * chans))
        for j in range(3):
            a_send[3 * i + j] = kernel_grad[:, j * chans : (j + 1) * chans].T
    sum_a.scatter()

    moving_g = [exchange(3, *ex_g[b], sc_g, rc_g) for b in range(count)]
    sums = []
    for b in range(count):
        arrive(moving_c[b], *ex_c[b], rc_c)
        widen_coarse(GC, b, rc_c)
        sums.append(backward_coarse(b))
        columns_fine(G, b, sc_g)
        send(moving_g[b])
        if b == 0:
            sum_a.scatter_rows()

    l_send[...] = jnp.concatenate(sums + [jnp.zeros((8 - count, chans), f32)], 0)
    l_moving = [
        remote(l_send, l_r1.at[2 * row + core], l_ssem.at[0], l_rsem.at[0],
               (lax.rem(row + at // 2, nr), twin if at % 2 else col))
        for at in range(1, 2 * nr)
    ]
    every = l_r1.at[pl.ds(0, 2 * nr - 1)]
    l_moving = l_moving, remote(every, every, l_ssem.at[0], l_rsem.at[0], (row, twin))
    send(l_moving)
    l_r1[2 * row + core] = l_send[...]

    for i in range(3):
        kernel_grad = jnp.zeros((2 * chans, 4 * chans), f32)
        for b in range(count):
            grad = G[b, 1 : tall + 1, :, chans : 3 * chans].reshape(tall * half, 2 * chans)
            kernel_grad = kernel_grad + outer(grad, V[b, i : i + tall].reshape(tall * half, 4 * chans))
        for j in range(3):
            both = kernel_grad[:chans, j * chans : (j + 1) * chans]
            both = both + kernel_grad[chans:, (j + 1) * chans : (j + 2) * chans]
            b_send[3 * i + j] = both.astype(bf16)
        if i == 1:
            sum_b.scatter(0)
    b_send[9] = jnp.zeros(b_send.shape[1:], bf16)
    sum_b.scatter(1)

    arrive(moving_g[0], *ex_g[0], rc_g)
    widen_fine(G, 0, rc_g)
    sum_a.cross()
    backward_fine(0, 0, 2)
    backward_fine(0, 1, 2)
    l_moving[1].wait_recv()
    total = l_r1[0]
    for at in range(1, 2 * nr):
        total = total + l_r1[at]
    l_s2[...] = total
    l_r2[pair] = total
    l_moving2 = [
        remote(l_s2, l_r2.at[pair], l_ssem.at[1], l_rsem.at[1],
               (row, lax.rem(pair + d, pairs) * 2 + core))
        for d in range(1, pairs)
    ]
    every = l_r2.at[pl.ds(0, pairs - 1)]
    l_moving2 = l_moving2, remote(every, every, l_ssem.at[1], l_rsem.at[1], (row, twin))
    send(l_moving2)

    arrive(moving_g[1], *ex_g[1], rc_g)
    widen_fine(G, 1, rc_g)
    backward_fine(1, 0, 2)
    sum_b.cross()
    backward_fine(1, 1, 2)
    sum_a.gather()
    sum_b.gather()
    sum_a.gather_cores()

    l_moving2[1].wait_recv()
    total = l_r2[0]
    for d in range(1, pairs):
        total = total + l_r2[d]
    l_send_done = pltpu.make_async_copy(l_f, l_out, out_sem.at[len(stores)])
    l_f[...] = total
    l_send_done.start()
    stores.append(l_send_done)
    sum_a.finish()
    stores.append(pltpu.make_async_copy(a_f, a_out, out_sem.at[len(stores)]))
    stores[-1].start()
    for c in sending:
        c.wait_send()
    sum_b.finish()
    stores.append(pltpu.make_async_copy(b_f, b_out, out_sem.at[len(stores)]))
    stores[-1].start()
    for c in stores:
        c.wait()


def finishing(
    factor, parts, times_in, grad_in, a_in, b_in, l_in, grad_out, fine_out, coarse_out, lift_out, table_out,
    times, g16, a16, b16, l32, g32, fine, coarse, lift, table, in_sem, out_sem,
):
    count, tall, chans = g16.shape[0], g16.shape[1], g16.shape[3]
    each = tall // parts
    pieces = [(b, pl.ds(p * each, each)) for b in range(count) for p in range(parts)]
    loads = [pltpu.make_async_copy(grad_in.at[b, rows], g16.at[b, rows], in_sem.at[4 + at])
             for at, (b, rows) in enumerate(pieces)]
    loads += [pltpu.make_async_copy(times_in, times, in_sem.at[3]), pltpu.make_async_copy(l_in, l32, in_sem.at[0]), pltpu.make_async_copy(b_in, b16, in_sem.at[1]),
              pltpu.make_async_copy(a_in, a16, in_sem.at[2])]
    for c in loads:
        c.start()
    stores = []

    def store(src, dst):
        stores.append(pltpu.make_async_copy(src, dst, out_sem.at[len(stores)]))
        stores[-1].start()

    for at, (b, rows) in enumerate(pieces):
        loads[at].wait()
        g32[b, rows] = g16[b, rows].astype(f32)
        store(g32.at[b, rows], grad_out.at[b, rows])
    loads[-4].wait()
    loads[-3].wait()
    total = factor * l32[...]
    ids = lax.broadcasted_iota(jnp.int32, table.shape, 0)
    placed = jnp.zeros(table.shape, f32)
    for b in range(count):
        placed = placed + jnp.where(ids == times[b], total[b : b + 1, :], 0.0)
    table[...] = placed
    store(table, table_out)
    loads[-2].wait()
    for t in range(9):
        fine[t // 3, t % 3] = factor * b16[t].astype(f32).T
    store(fine, fine_out)
    loads[-1].wait()
    for t in range(9):
        coarse[t // 3, t % 3] = factor * a16[t].astype(f32)
    store(coarse, coarse_out)
    lift[0:chans, :] = factor * a16[9, :, 0:chans].astype(f32)
    lift[chans : 2 * chans, :] = factor * a16[9, :, chans : 2 * chans].astype(f32)
    store(lift, lift_out)
    for c in stores:
        c.wait()


def solution(mesh):
    nr, nc = mesh.shape["row"], mesh.shape["col"]

    def body(latents, timesteps, time_table, conv_fine, conv_coarse, lift, cotangent):
        count, tall, broad, chans = latents.shape
        half, low = broad // 2, tall // 2
        share, pairs = chans // nr, nc // 2
        factor = 1.0 / math.sqrt(count * tall * broad * nr * nc)
        vm = pltpu.VMEM
        dma = pltpu.SemaphoreType.DMA
        hbm = pl.BlockSpec(memory_space=pl.ANY)

        def reducer(wide, peers, kind):
            return [
                vm((10, chans, wide), kind),
                vm((peers, 5, share, wide), bf16),
                vm((5, share, wide), bf16),
                vm((pairs, 5, share, wide), bf16),
                vm((5, share, wide), bf16),
                vm((10, chans, wide), bf16),
            ]

        def columns(n, wide):
            return [vm((count, 2, n, wide), f32), vm((count, 2, n + 16, wide), f32)]

        scratch = [
            pltpu.SMEM(timesteps.shape, jnp.int32), vm(latents.shape, bf16), vm(cotangent.shape, bf16), vm(time_table.shape, f32),
            vm(conv_fine.shape, bf16), vm(conv_coarse.shape, bf16), vm(lift.shape, f32),
            vm((12 * chans, 2 * chans), bf16), vm((12 * chans, 2 * chans), bf16), vm((18 * chans, chans), bf16),
            vm((2 * chans, 2 * chans), bf16), vm((chans, 2 * chans), bf16),
            vm((count, tall + 2, half, 4 * chans), bf16),
            vm((count, tall, half, 2 * chans), bf16),
            vm((count, tall, half, 2 * chans), f32),
            vm((count, low + 2, half, 3 * chans), bf16),
            vm((count, low, half, 2 * chans), bf16),
            vm((count, low * half, 2 * chans), f32),
            vm((count, low * half, 2 * chans), bf16),
            vm((count, low + 2, half, 6 * chans), bf16),
            vm((count, tall + 2, half, 4 * chans), bf16),
            vm(latents.shape, bf16),
            *columns(tall, chans), *columns(low, chans), *columns(low, 2 * chans), *columns(tall, chans),
            vm((5, chans, 2 * chans), f32), vm((5, chans, 2 * chans), bf16),
            *reducer(2 * chans, nr, f32), *reducer(chans, 2 * nr, bf16),
            vm((8, chans), f32), vm((2 * nr, 8, chans), f32), vm((8, chans), f32), vm((pairs, 8, chans), f32),
            vm((8, chans), f32),
        ]
        scratch += [dma((9,)), dma((7,)), dma((4 * count,)), dma((4 * count,)), dma((5,)), dma((5,)),
                    dma((5,)), dma((5,)), dma((2,)), dma((2,))]
        shape = jax.ShapeDtypeStruct
        grad, sum_a, sum_b, sum_l = pl.pallas_call(
            functools.partial(kernel, (nr, nc)),
            out_shape=[shape(latents.shape, bf16), shape((10, chans, 2 * chans), bf16),
                       shape((10, chans, chans), bf16), shape((8, chans), f32)],
            in_specs=[hbm] * 7,
            out_specs=[hbm] * 4,
            scratch_shapes=scratch,
            compiler_params=pltpu.CompilerParams(
                collective_id=0, has_side_effects=True, vmem_limit_bytes=60 * 2**20),
        )(timesteps, latents, cotangent, time_table, conv_fine, conv_coarse, lift)

        parts = 4
        results = [latents.shape, conv_fine.shape, conv_coarse.shape, lift.shape, time_table.shape]
        return pl.pallas_call(
            functools.partial(finishing, factor, parts),
            out_shape=[shape(s, f32) for s in results],
            in_specs=[hbm] * 5,
            out_specs=[hbm] * 5,
            scratch_shapes=[
                pltpu.SMEM(timesteps.shape, jnp.int32), vm(latents.shape, bf16), vm(sum_a.shape, bf16), vm(sum_b.shape, bf16), vm(sum_l.shape, f32),
                *[vm(s, f32) for s in results], dma((4 + count * parts,)), dma((4 + count * parts,))],
            compiler_params=pltpu.CompilerParams(vmem_limit_bytes=60 * 2**20),
        )(timesteps, grad, sum_a, sum_b, sum_l)

    in_specs = (P(None, "row", "col", None), P(), P(), P(), P(), P(), P(None, "row", "col", None))
    out_specs = (P(None, "row", "col", None), P(), P(), P(), P())
    return jax.shard_map(body, mesh=mesh, in_specs=in_specs, out_specs=out_specs, check_vma=False)
```

```python
import functools
import math

import jax
import jax.numpy as jnp
from jax import lax
from jax.experimental import pallas as pl
from jax.experimental.pallas import tpu as pltpu
from jax.sharding import PartitionSpec as P

MESH = pl.DeviceIdType.MESH
f32 = jnp.float32
bf16 = jnp.bfloat16


def dot(a, b):
    return jnp.dot(a, b, preferred_element_type=f32)


def outer(a, b):
    return lax.dot_general(a, b, (((0,), (0,)), ((), ())), preferred_element_type=f32)


def sigmoid(v):
    return 0.5 + 0.5 * jnp.tanh(0.5 * v)


def shifted(v, column, step):
    n = v.shape[1]
    ids = lax.broadcasted_iota(jnp.int32, v.shape, 1)
    edge = 0 if step == 1 else n - 1
    return jnp.where(ids == edge, column[:, None, :], pltpu.roll(v, step % n, 1))


def kernel(
    sizes,
    times_in, lat_in, cot_in, table_in, fine_in, coarse_in, lift_in,
    grad_out, a_out, b_out, l_out,
    times, lat, cot, table, kfine, kcoarse, lift,
    w_fwd, w_back, wc_back, lift_hi, lift_lo,
    V, C2, SL, PO, UG, CB, ACT, GC, G, OUT,
    sc_v, rc_v, sc_p, rc_p, sc_c, rc_c, sc_g, rc_g, er_p, er_c,
    a_theirs, a_mixed, a_send, a_r1, a_s2, a_r2, a_t, a_f,
    b_send, b_r1, b_s2, b_r2, b_t, b_f,
    l_send, l_r1, l_s2, l_r2, l_f,
    in_sem, out_sem, h_ssem, h_rsem, a_ssem, a_rsem, b_ssem, b_rsem, l_ssem, l_rsem,
):
    nr, nc = sizes
    pairs = nc // 2
    row, col = lax.axis_index("row"), lax.axis_index("col")
    core, pair = lax.rem(col, 2), col // 2
    twin = col + 1 - 2 * core
    up, down = lax.rem(row + nr - 1, nr), lax.rem(row + 1, nr)
    left, right = lax.rem(col + nc - 1, nc), lax.rem(col + 1, nc)
    other = jnp.where(core == 0, left, right)
    count, tall, half = C2.shape[0], C2.shape[1], C2.shape[2]
    low = tall // 2
    chans = lat.shape[3]

    barrier = pltpu.get_barrier_semaphore()
    partners = [(lax.rem(row + d, nr), col) for d in range(1, nr)]
    partners += [(lax.rem(row + d, nr), twin) for d in range(nr)]
    partners += [(row, lax.rem(pair + d, pairs) * 2 + core) for d in range(1, pairs)]
    partners += [(up, other), (row, other), (down, other)]
    for who in partners:
        pl.semaphore_signal(barrier, inc=1, device_id=who, device_id_type=MESH)

    loads = {}

    def load(name, src, dst):
        loads[name] = pltpu.make_async_copy(src, dst, in_sem.at[len(loads)])
        loads[name].start()

    load("lat0", lat_in.at[0], lat.at[0])
    load("lat1", lat_in.at[1], lat.at[1])
    load("kfine", fine_in, kfine)
    load("times", times_in, times)

    sending = []

    def remote(src, dst, ssem, rsem, who):
        return pltpu.make_async_remote_copy(
            src_ref=src, dst_ref=dst, send_sem=ssem, recv_sem=rsem, device_id=who, device_id_type=MESH)

    def exchange(kind, b, buf, n, lo, hi, sc, rc, edges=None):
        at = kind * count + b
        first_col, last_col = sc.at[b, 0], sc.at[b, 1]
        to_left, to_right = rc.at[b, 1], rc.at[b, 0]
        lanes = pl.ds(lo, hi - lo)
        first_row, last_row = buf.at[b, 1, :, lanes], buf.at[b, n, :, lanes]
        if edges is not None:
            first_row, last_row = edges.at[b, 0], edges.at[b, 1]
        plan = [
            (first_col.at[pl.ds(0, 8)], to_left.at[pl.ds(n + 8, 8)], (up, left)),
            (last_col.at[pl.ds(0, 8)], to_right.at[pl.ds(n + 8, 8)], (up, right)),
            (first_col.at[pl.ds(n - 8, 8)], to_left.at[pl.ds(0, 8)], (down, left)),
            (last_col.at[pl.ds(n - 8, 8)], to_right.at[pl.ds(0, 8)], (down, right)),
            (first_col, to_left.at[pl.ds(8, n)], (row, left)),
            (last_col, to_right.at[pl.ds(8, n)], (row, right)),
            (first_row, buf.at[b, n + 1, :, lanes], (up, col)),
            (last_row, buf.at[b, 0, :, lanes], (down, col)),
        ]
        rows = sum(math.prod(src.shape) * jnp.dtype(src.dtype).itemsize for src, _, _ in plan) // (4 * chans)
        every = table.at[pl.ds(0, rows)]
        return ([remote(src, dst, h_ssem.at[at], h_rsem.at[at], who) for src, dst, who in plan],
                remote(every, every, h_ssem.at[at], h_rsem.at[at], (row, twin)))

    def send(copies):
        for c in copies[0]:
            c.start()
        sending.append(copies[1])

    def arrive(copies, b, buf, n, lo, hi, rc):
        copies[1].wait_recv()
        nothing = jnp.zeros((buf.shape[2], hi - lo), buf.dtype)

        @pl.when(row == 0)
        def _():
            buf[b, 0, :, lo:hi] = nothing
            rc[b, :, 0:8, :] = jnp.zeros((2, 8, rc.shape[3]), f32)

        @pl.when(row == nr - 1)
        def _():
            buf[b, n + 1, :, lo:hi] = nothing
            rc[b, :, n + 8 : n + 16, :] = jnp.zeros((2, 8, rc.shape[3]), f32)

        @pl.when(col == 0)
        def _():
            rc[b, 0] = jnp.zeros(rc.shape[2:], f32)

        @pl.when(col == nc - 1)
        def _():
            rc[b, 1] = jnp.zeros(rc.shape[2:], f32)

    def widen_fine(buf, b, rc):
        before, after = rc[b, 0, 7 : 7 + tall + 2, :], rc[b, 1, 7 : 7 + tall + 2, :]
        odd = buf[b, :, :, 2 * chans : 3 * chans].astype(f32)
        buf[b, :, :, 0:chans] = shifted(odd, before, 1).astype(bf16)
        even = buf[b, :, :, chans : 2 * chans].astype(f32)
        buf[b, :, :, 3 * chans : 4 * chans] = shifted(even, after, -1).astype(bf16)

    def widen_coarse(buf, b, rc):
        wide_by = rc.shape[3]
        before, after = rc[b, 0, 7 : 7 + low + 2, :], rc[b, 1, 7 : 7 + low + 2, :]
        mid = buf[b, :, :, wide_by : 2 * wide_by].astype(f32)
        buf[b, :, :, 0:wide_by] = shifted(mid, before, 1).astype(bf16)
        buf[b, :, :, 2 * wide_by : 3 * wide_by] = shifted(mid, after, -1).astype(bf16)

    def columns_fine(buf, b, sc):
        sc[b, 0] = buf[b, 1 : tall + 1, 0:16, chans : 2 * chans].astype(f32)[:, 0, :]
        sc[b, 1] = buf[b, 1 : tall + 1, half - 16 : half, 2 * chans : 3 * chans].astype(f32)[:, 15, :]

    def split_latents(b):
        V[b, 1 : tall + 1, :, chans : 3 * chans] = lat[b].reshape(tall, half, 2 * chans)

    def split_cotangent(b):
        def one(k, _):
            rows = pl.ds(k * 16, 16)
            both = cot[b, rows].reshape(16, half, 2 * chans)
            C2[b, rows] = both
            total = both.astype(f32).reshape(8, 2, half, 2 * chans).sum(axis=1)
            total = total[:, :, :chans] + total[:, :, chans:]
            upper = total.astype(bf16)
            rest = (total - upper.astype(f32)).astype(bf16)
            UG[b, pl.ds(k * 8, 8)] = jnp.concatenate([upper, rest], -1)
            return 0

        lax.fori_loop(0, tall // 16, one, 0)

    def prepare_forward():
        w_fwd[...] = jnp.zeros(w_fwd.shape, bf16)
        for i in range(3):
            base = i * 4 * chans
            for part in range(2):
                for j in range(3):
                    at = base + (part + j) * chans
                    w_fwd[at : at + chans, part * chans : (part + 1) * chans] = kfine[i, j]

    def prepare_back():
        w_back[...] = jnp.zeros(w_back.shape, bf16)
        for i in range(3):
            for j in range(3):
                turned = kfine[i, j].T
                for part in range(2):
                    at = i * 4 * chans + (part + 2 - j) * chans
                    w_back[at : at + chans, part * chans : (part + 1) * chans] = turned
                at = (i * 3 + 2 - j) * 2 * chans
                wc_back[at : at + 2 * chans, :] = kcoarse[i, j].T

    def prepare_lift():
        turned = lift[...].T
        upper = turned.astype(bf16)
        lift_hi[0:chans, :] = upper
        lift_hi[chans : 2 * chans, :] = upper
        lift_lo[...] = (turned - upper.astype(f32)).astype(bf16)

    def lift_back(b):
        ug = UG[b].reshape(low * half, 2 * chans)
        CB[b] = dot(ug, lift_hi[...]) + dot(ug[:, :chans], lift_lo[...])

    def forward_fine(b):
        embedding = table[pl.ds(times[b], 1), :]
        embedding = jnp.concatenate([embedding, embedding], -1)
        step = 32

        def one(k, _):
            taps = [V[b, pl.ds(k * step + i, step)].reshape(step * half, 4 * chans) for i in range(3)]
            pre = dot(jnp.concatenate(taps, -1), w_fwd[...]) + embedding
            s = sigmoid(pre)
            hidden = pre * s
            SL[b, pl.ds(k * step, step)] = (s + hidden * (1.0 - s)).reshape(step, half, 2 * chans)
            hidden = hidden.astype(bf16).astype(f32).reshape(step // 2, 2, half, 2 * chans).sum(axis=1)
            pooled = 0.25 * (hidden[:, :, :chans] + hidden[:, :, chans:])
            PO[b, pl.ds(k * (step // 2) + 1, step // 2), :, chans : 2 * chans] = pooled.astype(bf16)
            return 0

        lax.fori_loop(0, tall // step, one, 0)

    def border_columns(buf, b, n):
        strips = []
        for at in (0, 15):
            lo = at // 15 * (half - 16)
            strip = buf[b, :, lo : lo + 16, :].astype(f32)[:, at, :]
            strips.append(jnp.concatenate([strip[i : i + n] for i in range(3)], -1).astype(bf16))
        return strips

    def border_rows(buf, b, first, rows):
        taps = [buf[b, first + i : first + i + rows].reshape(rows * half, buf.shape[3]) for i in range(3)]
        return jnp.concatenate(taps, -1)

    def fine_border(b):
        embedding = table[pl.ds(times[b], 1), :]
        embedding = jnp.concatenate([embedding, embedding], -1)
        taps = border_columns(V, b, tall) + [border_rows(V, b, 0, 2), border_rows(V, b, tall - 2, 2)]
        pre = dot(jnp.concatenate(taps, 0), w_fwd[...]) + embedding
        hidden = (pre * sigmoid(pre)).astype(bf16).astype(f32)
        across = hidden[: 2 * tall].reshape(2 * low, 2, 2 * chans).sum(axis=1)
        across = (0.25 * (across[:, :chans] + across[:, chans:])).astype(bf16).astype(f32)
        sc_p[b, 0], sc_p[b, 1] = across[:low], across[low:]
        along = hidden[2 * tall :].reshape(2, 2, half, 2 * chans).sum(axis=1)
        er_p[b] = (0.25 * (along[:, :, :chans] + along[:, :, chans:])).astype(bf16)

    def coarse_border(b):
        taps = border_columns(PO, b, low) + [border_rows(PO, b, 0, 1), border_rows(PO, b, low - 1, 1)]
        pre = dot(jnp.concatenate(taps, 0), kcoarse[...].reshape(9 * chans, 2 * chans))
        s = sigmoid(pre)
        back = CB[b].reshape(low, half, 2 * chans)
        back = [back[:, 0, :], back[:, half - 1, :], back[0], back[low - 1]]
        grad = jnp.concatenate(back, 0) * (s + pre * s * (1.0 - s))
        grad = grad.astype(bf16)
        sc_c[b, 0], sc_c[b, 1] = grad[:low].astype(f32), grad[low : 2 * low].astype(f32)
        er_c[b, 0], er_c[b, 1] = grad[2 * low : 2 * low + half], grad[2 * low + half :]

    def forward_coarse(b):
        step = 32

        def one(k, _):
            flat = step * half
            taps = [PO[b, pl.ds(k * step + i, step)].reshape(flat, 3 * chans) for i in range(3)]
            weights = kcoarse[...].reshape(9 * chans, 2 * chans)
            pre = dot(jnp.concatenate(taps, -1), weights)
            s = sigmoid(pre)
            act = pre * s
            here = pl.ds(pl.multiple_of(k * flat, flat), flat)
            ACT[b, here, :] = act.astype(bf16)
            grad = (CB[b, here, :] * (s + act * (1.0 - s))).astype(bf16)
            GC[b, pl.ds(k * step + 1, step), :, 2 * chans : 4 * chans] = grad.reshape(step, half, 2 * chans)
            return 0

        lax.fori_loop(0, low // step, one, 0)

    def backward_coarse(b):
        step = 32

        def one(k, total):
            flat = step * half
            taps = [GC[b, pl.ds(k * step + 2 - i, step)].reshape(flat, 6 * chans) for i in range(3)]
            pooled = 0.25 * dot(jnp.concatenate(taps, -1), wc_back[...])
            pooled = pooled.reshape(step, 1, half, chans)
            pooled = jnp.concatenate([pooled, pooled], -1)
            rows = pl.ds(k * 2 * step, 2 * step)
            direct = C2[b, rows].astype(f32).reshape(step, 2, half, 2 * chans)
            slope = SL[b, rows].reshape(step, 2, half, 2 * chans)
            grad = ((direct + pooled) * slope).astype(bf16)
            G[b, pl.ds(k * 2 * step + 1, 2 * step), :, chans : 3 * chans] = grad.reshape(2 * step, half, 2 * chans)
            return total + grad.astype(f32).reshape(2 * flat // 8, 8, 2 * chans).sum(axis=0)

        total = lax.fori_loop(0, low // step, one, jnp.zeros((8, 2 * chans), f32))
        total = total[:, :chans] + total[:, chans:]
        return total.sum(axis=0, keepdims=True)

    stores = []

    def backward_fine(b, part, parts):
        step = 32

        def one(k, _):
            taps = [G[b, pl.ds(k * step + 2 - i, step)].reshape(step * half, 4 * chans) for i in range(3)]
            grad = dot(jnp.concatenate(taps, -1), w_back[...]).astype(bf16)
            OUT[b, pl.ds(k * step, step)] = grad.reshape(step, 2 * half, chans)
            return 0

        each = tall // step // parts
        lax.fori_loop(part * each, (part + 1) * each, one, 0)
        rows = pl.ds(part * each * step, each * step)
        stores.append(pltpu.make_async_copy(OUT.at[b, rows], grad_out.at[b, rows], out_sem.at[len(stores)]))
        stores[-1].start()

    class Reduce:
        def __init__(self, mine, first, part, second, owned, full, ssem, rsem):
            self.refs = mine, first, part, second, owned, full
            self.ssem, self.rsem = ssem, rsem
            self.share, self.half = chans // nr, mine.shape[0] // 2
            self.peers = first.shape[0] - 1

        def all_of(self, phase):
            every = self.refs[3].at[pl.ds(0, pairs - 1)] if phase == 2 else self.refs[1].at[pl.ds(1, self.peers)]
            return remote(every, every, self.ssem.at[phase], self.rsem.at[phase], (row, twin))

        def rows_of(self, peer):
            return pl.ds(pl.multiple_of(peer * self.share, self.share), self.share)

        def chunk(self, ref, owner_core, peer):
            return ref.at[pl.ds(owner_core * self.half, self.half), self.rows_of(peer)]

        def copy1(self, d, to_core):
            mine, first = self.refs[:2]
            peer, flip = lax.rem(row + d, nr), lax.rem(core + to_core, 2)
            return remote(self.chunk(mine, to_core, peer), first.at[2 * d + flip],
                          self.ssem.at[1], self.rsem.at[1], (peer, 2 * pair + to_core))

        def scatter(self, to_core):
            pl.when(core != to_core)(self.copy1(0, to_core).start)
            for d in range(1, nr):
                self.copy1(d, to_core).start()

        def copy2(self, d):
            _, _, part, second = self.refs[:4]
            return remote(part, second.at[pair], self.ssem.at[2], self.rsem.at[2],
                          (row, lax.rem(pair + d, pairs) * 2 + core))

        def cross(self):
            mine, first, part, second = self.refs[:4]
            self.all_of(1).wait_recv()
            total = mine[pl.ds(core * self.half, self.half), self.rows_of(row), :].astype(f32)
            for at in range(1, 2 * nr):
                total = total + first[at].astype(f32)
            part[...] = total.astype(bf16)
            second[pair] = total.astype(bf16)
            for d in range(1, pairs):
                self.copy2(d).start()

        def copy3(self, d, flip):
            owned, full = self.refs[4:]
            peer = lax.rem(row + d, nr)
            return remote(owned, self.chunk(full, core, row), self.ssem.at[3], self.rsem.at[3],
                          (peer, twin if flip else col))

        def collect(self):
            second, owned, full = self.refs[3:]
            self.all_of(2).wait_recv()
            total = second[0].astype(f32)
            for at in range(1, pairs):
                total = total + second[at].astype(f32)
            owned[...] = total.astype(bf16)
            full[pl.ds(core * self.half, self.half), self.rows_of(row), :] = total.astype(bf16)

        def gather(self):
            self.collect()
            for at in range(1, 2 * nr):
                self.copy3(at // 2, at % 2).start()

        def finish(self):
            self.all_of(3).wait_recv()
            for phase in range(1, 4):
                self.all_of(phase).wait_send()

    class ReduceByChip(Reduce):
        def __init__(self, theirs, mixed, *rest):
            super().__init__(*rest)
            self.theirs, self.mixed = theirs, mixed

        def copy0(self):
            give = self.refs[0].at[pl.ds((1 - core) * self.half, self.half)]
            return remote(give, self.theirs, self.ssem.at[0], self.rsem.at[0], (row, twin))

        def copy1(self, d):
            peer = lax.rem(row + d, nr)
            return remote(self.mixed.at[:, self.rows_of(peer)], self.refs[1].at[d],
                          self.ssem.at[1], self.rsem.at[1], (peer, col))

        def scatter(self):
            self.copy0().start()

        def scatter_rows(self):
            self.copy0().wait_recv()
            total = self.refs[0][pl.ds(core * self.half, self.half)] + self.theirs[...]
            self.mixed[...] = total.astype(bf16)
            for d in range(1, nr):
                self.copy1(d).start()

        def cross(self):
            _, first, part, second = self.refs[:4]
            self.all_of(1).wait_recv()
            total = self.mixed[:, self.rows_of(row), :].astype(f32)
            for d in range(1, nr):
                total = total + first[d].astype(f32)
            part[...] = total.astype(bf16)
            second[pair] = total.astype(bf16)
            for d in range(1, pairs):
                self.copy2(d).start()

        def gather(self):
            self.collect()
            for d in range(1, nr):
                self.copy3(d, 0).start()

        def copy4(self):
            done = self.refs[5].at[pl.ds(core * self.half, self.half)]
            return remote(done, done, self.ssem.at[4], self.rsem.at[4], (row, twin))

        def gather_cores(self):
            self.all_of(3).wait_recv()
            self.copy4().start()

        def finish(self):
            self.copy4().wait()
            self.copy0().wait_send()
            for phase in range(1, 4):
                self.all_of(phase).wait_send()

    sum_a = ReduceByChip(a_theirs, a_mixed, a_send, a_r1, a_s2, a_r2, a_t, a_f, a_ssem, a_rsem)
    sum_b = Reduce(b_send, b_r1, b_s2, b_r2, b_t, b_f, b_ssem, b_rsem)

    ex_v = [(b, V, tall, chans, 3 * chans) for b in range(count)]
    ex_p = [(b, PO, low, chans, 2 * chans) for b in range(count)]
    ex_c = [(b, GC, low, 2 * chans, 4 * chans) for b in range(count)]
    ex_g = [(b, G, tall, chans, 3 * chans) for b in range(count)]
    loads["lat0"].wait()
    split_latents(0)
    columns_fine(V, 0, sc_v)
    pl.semaphore_wait(barrier, len(partners))
    moving_v = [exchange(0, *ex_v[b], sc_v, rc_v) for b in range(count)]
    send(moving_v[0])
    loads["lat1"].wait()
    split_latents(1)
    columns_fine(V, 1, sc_v)
    send(moving_v[1])
    load("table", table_in, table)
    load("cot0", cot_in.at[0], cot.at[0])
    load("cot1", cot_in.at[1], cot.at[1])
    load("lift", lift_in, lift)
    load("kcoarse", coarse_in, kcoarse)
    loads["kfine"].wait()
    prepare_forward()
    loads["cot0"].wait()
    split_cotangent(0)
    loads["cot1"].wait()
    split_cotangent(1)
    loads["lift"].wait()
    prepare_lift()
    lift_back(0)
    lift_back(1)
    loads["kcoarse"].wait()
    prepare_back()
    loads["table"].wait()
    loads["times"].wait()

    moving_p = [exchange(1, *ex_p[b], sc_p, rc_p, er_p) for b in range(count)]
    for b in range(count):
        arrive(moving_v[b], *ex_v[b], rc_v)
        widen_fine(V, b, rc_v)
        fine_border(b)
        send(moving_p[b])
    for b in range(count):
        forward_fine(b)

    moving_c = [exchange(2, *ex_c[b], sc_c, rc_c, er_c) for b in range(count)]
    for b in range(count):
        arrive(moving_p[b], *ex_p[b], rc_p)
        widen_coarse(PO, b, rc_p)
        coarse_border(b)
        send(moving_c[b])
    for b in range(count):
        forward_coarse(b)

    lifted = jnp.zeros((2 * chans, 2 * chans), f32)
    for b in range(count):
        lifted = lifted + outer(ACT[b], UG[b].reshape(low * half, 2 * chans))
    lifted = lifted[:, :chans] + lifted[:, chans:]
    a_send[9, :, 0:chans] = lifted[:chans]
    a_send[9, :, chans : 2 * chans] = lifted[chans:]
    for i in range(3):
        kernel_grad = jnp.zeros((2 * chans, 3 * chans), f32)
        for b in range(count):
            grad = GC[b, 1 : low + 1, :, 2 * chans : 4 * chans].reshape(low * half, 2 * chans)
            kernel_grad = kernel_grad + outer(grad, PO[b, i : i + low].reshape(low * half, 3 * chans))
        for j in range(3):
            a_send[3 * i + j] = kernel_grad[:, j * chans : (j + 1) * chans].T
    sum_a.scatter()

    moving_g = [exchange(3, *ex_g[b], sc_g, rc_g) for b in range(count)]
    sums = []
    for b in range(count):
        arrive(moving_c[b], *ex_c[b], rc_c)
        widen_coarse(GC, b, rc_c)
        sums.append(backward_coarse(b))
        columns_fine(G, b, sc_g)
        send(moving_g[b])
        if b == 0:
            sum_a.scatter_rows()

    l_send[...] = jnp.concatenate(sums + [jnp.zeros((8 - count, chans), f32)], 0)
    l_moving = [
        remote(l_send, l_r1.at[2 * row + core], l_ssem.at[0], l_rsem.at[0],
               (lax.rem(row + at // 2, nr), twin if at % 2 else col))
        for at in range(1, 2 * nr)
    ]
    every = l_r1.at[pl.ds(0, 2 * nr - 1)]
    l_moving = l_moving, remote(every, every, l_ssem.at[0], l_rsem.at[0], (row, twin))
    send(l_moving)
    l_r1[2 * row + core] = l_send[...]

    for i in range(3):
        kernel_grad = jnp.zeros((2 * chans, 4 * chans), f32)
        for b in range(count):
            grad = G[b, 1 : tall + 1, :, chans : 3 * chans].reshape(tall * half, 2 * chans)
            kernel_grad = kernel_grad + outer(grad, V[b, i : i + tall].reshape(tall * half, 4 * chans))
        for j in range(3):
            both = kernel_grad[:chans, j * chans : (j + 1) * chans]
            both = both + kernel_grad[chans:, (j + 1) * chans : (j + 2) * chans]
            b_send[3 * i + j] = both.astype(bf16)
        if i == 1:
            sum_b.scatter(0)
    b_send[9] = jnp.zeros(b_send.shape[1:], bf16)
    sum_b.scatter(1)

    arrive(moving_g[0], *ex_g[0], rc_g)
    widen_fine(G, 0, rc_g)
    sum_a.cross()
    backward_fine(0, 0, 2)
    backward_fine(0, 1, 2)
    l_moving[1].wait_recv()
    total = l_r1[0]
    for at in range(1, 2 * nr):
        total = total + l_r1[at]
    l_s2[...] = total
    l_r2[pair] = total
    l_moving2 = [
        remote(l_s2, l_r2.at[pair], l_ssem.at[1], l_rsem.at[1],
               (row, lax.rem(pair + d, pairs) * 2 + core))
        for d in range(1, pairs)
    ]
    every = l_r2.at[pl.ds(0, pairs - 1)]
    l_moving2 = l_moving2, remote(every, every, l_ssem.at[1], l_rsem.at[1], (row, twin))
    send(l_moving2)

    arrive(moving_g[1], *ex_g[1], rc_g)
    widen_fine(G, 1, rc_g)
    backward_fine(1, 0, 2)
    sum_b.cross()
    backward_fine(1, 1, 2)
    sum_a.gather()
    sum_b.gather()
    sum_a.gather_cores()

    l_moving2[1].wait_recv()
    total = l_r2[0]
    for d in range(1, pairs):
        total = total + l_r2[d]
    l_send_done = pltpu.make_async_copy(l_f, l_out, out_sem.at[len(stores)])
    l_f[...] = total
    l_send_done.start()
    stores.append(l_send_done)
    sum_a.finish()
    stores.append(pltpu.make_async_copy(a_f, a_out, out_sem.at[len(stores)]))
    stores[-1].start()
    for c in sending:
        c.wait_send()
    sum_b.finish()
    stores.append(pltpu.make_async_copy(b_f, b_out, out_sem.at[len(stores)]))
    stores[-1].start()
    for c in stores:
        c.wait()


def finishing(
    factor, parts, times_in, grad_in, a_in, b_in, l_in, grad_out, fine_out, coarse_out, lift_out, table_out,
    times, g16, a16, b16, l32, g32, fine, coarse, lift, table, in_sem, out_sem,
):
    count, tall, chans = g16.shape[0], g16.shape[1], g16.shape[3]
    each = tall // parts
    pieces = [(b, pl.ds(p * each, each)) for b in range(count) for p in range(parts)]
    loads = [pltpu.make_async_copy(grad_in.at[b, rows], g16.at[b, rows], in_sem.at[4 + at])
             for at, (b, rows) in enumerate(pieces)]
    loads += [pltpu.make_async_copy(times_in, times, in_sem.at[3]), pltpu.make_async_copy(l_in, l32, in_sem.at[0]), pltpu.make_async_copy(b_in, b16, in_sem.at[1]),
              pltpu.make_async_copy(a_in, a16, in_sem.at[2])]
    for c in loads:
        c.start()
    stores = []

    def store(src, dst):
        stores.append(pltpu.make_async_copy(src, dst, out_sem.at[len(stores)]))
        stores[-1].start()

    for at, (b, rows) in enumerate(pieces):
        loads[at].wait()
        g32[b, rows] = g16[b, rows].astype(f32)
        store(g32.at[b, rows], grad_out.at[b, rows])
    loads[-4].wait()
    loads[-3].wait()
    total = factor * l32[...]
    ids = lax.broadcasted_iota(jnp.int32, table.shape, 0)
    placed = jnp.zeros(table.shape, f32)
    for b in range(count):
        placed = placed + jnp.where(ids == times[b], total[b : b + 1, :], 0.0)
    table[...] = placed
    store(table, table_out)
    loads[-2].wait()
    for t in range(9):
        fine[t // 3, t % 3] = factor * b16[t].astype(f32).T
    store(fine, fine_out)
    loads[-1].wait()
    for t in range(9):
        coarse[t // 3, t % 3] = factor * a16[t].astype(f32)
    store(coarse, coarse_out)
    lift[0:chans, :] = factor * a16[9, :, 0:chans].astype(f32)
    lift[chans : 2 * chans, :] = factor * a16[9, :, chans : 2 * chans].astype(f32)
    store(lift, lift_out)
    for c in stores:
        c.wait()


def solution(mesh):
    nr, nc = mesh.shape["row"], mesh.shape["col"]

    def body(latents, timesteps, time_table, conv_fine, conv_coarse, lift, cotangent):
        count, tall, broad, chans = latents.shape
        half, low = broad // 2, tall // 2
        share, pairs = chans // nr, nc // 2
        factor = 1.0 / math.sqrt(count * tall * broad * nr * nc)
        vm = pltpu.VMEM
        dma = pltpu.SemaphoreType.DMA
        hbm = pl.BlockSpec(memory_space=pl.ANY)

        def reducer(wide, peers, kind):
            return [
                vm((10, chans, wide), kind),
                vm((peers, 5, share, wide), bf16),
                vm((5, share, wide), bf16),
                vm((pairs, 5, share, wide), bf16),
                vm((5, share, wide), bf16),
                vm((10, chans, wide), bf16),
            ]

        def columns(n, wide):
            return [vm((count, 2, n, wide), f32), vm((count, 2, n + 16, wide), f32)]

        scratch = [
            pltpu.SMEM(timesteps.shape, jnp.int32), vm(latents.shape, bf16), vm(cotangent.shape, bf16), vm(time_table.shape, f32),
            vm(conv_fine.shape, bf16), vm(conv_coarse.shape, bf16), vm(lift.shape, f32),
            vm((12 * chans, 2 * chans), bf16), vm((12 * chans, 2 * chans), bf16), vm((18 * chans, chans), bf16),
            vm((2 * chans, 2 * chans), bf16), vm((chans, 2 * chans), bf16),
            vm((count, tall + 2, half, 4 * chans), bf16),
            vm((count, tall, half, 2 * chans), bf16),
            vm((count, tall, half, 2 * chans), f32),
            vm((count, low + 2, half, 3 * chans), bf16),
            vm((count, low, half, 2 * chans), bf16),
            vm((count, low * half, 2 * chans), f32),
            vm((count, low * half, 2 * chans), bf16),
            vm((count, low + 2, half, 6 * chans), bf16),
            vm((count, tall + 2, half, 4 * chans), bf16),
            vm(latents.shape, bf16),
            *columns(tall, chans), *columns(low, chans), *columns(low, 2 * chans), *columns(tall, chans),
            vm((count, 2, half, chans), bf16), vm((count, 2, half, 2 * chans), bf16),
            vm((5, chans, 2 * chans), f32), vm((5, chans, 2 * chans), bf16),
            *reducer(2 * chans, nr, f32), *reducer(chans, 2 * nr, bf16),
            vm((8, chans), f32), vm((2 * nr, 8, chans), f32), vm((8, chans), f32), vm((pairs, 8, chans), f32),
            vm((8, chans), f32),
        ]
        scratch += [dma((9,)), dma((7,)), dma((4 * count,)), dma((4 * count,)), dma((5,)), dma((5,)),
                    dma((5,)), dma((5,)), dma((2,)), dma((2,))]
        shape = jax.ShapeDtypeStruct
        grad, sum_a, sum_b, sum_l = pl.pallas_call(
            functools.partial(kernel, (nr, nc)),
            out_shape=[shape(latents.shape, bf16), shape((10, chans, 2 * chans), bf16),
                       shape((10, chans, chans), bf16), shape((8, chans), f32)],
            in_specs=[hbm] * 7,
            out_specs=[hbm] * 4,
            scratch_shapes=scratch,
            compiler_params=pltpu.CompilerParams(
                collective_id=0, has_side_effects=True, vmem_limit_bytes=60 * 2**20),
        )(timesteps, latents, cotangent, time_table, conv_fine, conv_coarse, lift)

        parts = 4
        results = [latents.shape, conv_fine.shape, conv_coarse.shape, lift.shape, time_table.shape]
        return pl.pallas_call(
            functools.partial(finishing, factor, parts),
            out_shape=[shape(s, f32) for s in results],
            in_specs=[hbm] * 5,
            out_specs=[hbm] * 5,
            scratch_shapes=[
                pltpu.SMEM(timesteps.shape, jnp.int32), vm(latents.shape, bf16), vm(sum_a.shape, bf16), vm(sum_b.shape, bf16), vm(sum_l.shape, f32),
                *[vm(s, f32) for s in results], dma((4 + count * parts,)), dma((4 + count * parts,))],
            compiler_params=pltpu.CompilerParams(vmem_limit_bytes=60 * 2**20),
        )(timesteps, grad, sum_a, sum_b, sum_l)

    in_specs = (P(None, "row", "col", None), P(), P(), P(), P(), P(), P(None, "row", "col", None))
    out_specs = (P(None, "row", "col", None), P(), P(), P(), P())
    return jax.shard_map(body, mesh=mesh, in_specs=in_specs, out_specs=out_specs, check_vma=False)
```

```python
import functools
import math

import jax
import jax.numpy as jnp
from jax import lax
from jax.experimental import pallas as pl
from jax.experimental.pallas import tpu as pltpu
from jax.sharding import PartitionSpec as P

MESH = pl.DeviceIdType.MESH
f32 = jnp.float32
bf16 = jnp.bfloat16


def dot(a, b):
    return jnp.dot(a, b, preferred_element_type=f32)


def outer(a, b):
    return lax.dot_general(a, b, (((0,), (0,)), ((), ())), preferred_element_type=f32)


def sigmoid(v):
    return 0.5 + 0.5 * jnp.tanh(0.5 * v)


def shifted(v, column, step):
    n = v.shape[1]
    ids = lax.broadcasted_iota(jnp.int32, v.shape, 1)
    edge = 0 if step == 1 else n - 1
    return jnp.where(ids == edge, column[:, None, :], pltpu.roll(v, step % n, 1))


def kernel(
    sizes,
    times_in, lat_in, cot_in, table_in, fine_in, coarse_in, lift_in,
    grad_out, a_out, b_out, l_out,
    times, lat, cot, table, kfine, kcoarse, lift,
    w_fwd, w_back, wc_back, lift_hi, lift_lo,
    V, C2, SL, PO, UG, CB, ACT, GC, G, OUT,
    sc_v, rc_v, sc_p, rc_p, sc_c, rc_c, sc_g, rc_g, er_p, er_c,
    a_theirs, a_mixed, a_send, a_r1, a_s2, a_r2, a_t, a_f,
    b_send, b_r1, b_s2, b_r2, b_t, b_f,
    l_send, l_r1, l_s2, l_r2, l_f,
    in_sem, out_sem, h_ssem, h_rsem, a_ssem, a_rsem, b_ssem, b_rsem, l_ssem, l_rsem,
):
    nr, nc = sizes
    pairs = nc // 2
    row, col = lax.axis_index("row"), lax.axis_index("col")
    core, pair = lax.rem(col, 2), col // 2
    twin = col + 1 - 2 * core
    up, down = lax.rem(row + nr - 1, nr), lax.rem(row + 1, nr)
    left, right = lax.rem(col + nc - 1, nc), lax.rem(col + 1, nc)
    other = jnp.where(core == 0, left, right)
    count, tall, half = C2.shape[0], C2.shape[1], C2.shape[2]
    low = tall // 2
    chans = lat.shape[3]

    barrier = pltpu.get_barrier_semaphore()
    partners = [(lax.rem(row + d, nr), col) for d in range(1, nr)]
    partners += [(lax.rem(row + d, nr), twin) for d in range(nr)]
    partners += [(row, lax.rem(pair + d, pairs) * 2 + core) for d in range(1, pairs)]
    partners += [(up, other), (row, other), (down, other)]
    for who in partners:
        pl.semaphore_signal(barrier, inc=1, device_id=who, device_id_type=MESH)

    loads = {}

    def load(name, src, dst):
        loads[name] = pltpu.make_async_copy(src, dst, in_sem.at[len(loads)])
        loads[name].start()

    load("lat0", lat_in.at[0], lat.at[0])
    load("lat1", lat_in.at[1], lat.at[1])
    load("kfine", fine_in, kfine)
    load("times", times_in, times)

    sending = []

    def remote(src, dst, ssem, rsem, who):
        return pltpu.make_async_remote_copy(
            src_ref=src, dst_ref=dst, send_sem=ssem, recv_sem=rsem, device_id=who, device_id_type=MESH)

    def exchange(kind, b, buf, n, lo, hi, sc, rc, edges=None):
        at = kind * count + b
        first_col, last_col = sc.at[b, 0], sc.at[b, 1]
        to_left, to_right = rc.at[b, 1], rc.at[b, 0]
        lanes = pl.ds(lo, hi - lo)
        first_row, last_row = buf.at[b, 1, :, lanes], buf.at[b, n, :, lanes]
        if edges is not None:
            first_row, last_row = edges.at[b, 0], edges.at[b, 1]
        plan = [
            (first_col.at[pl.ds(0, 8)], to_left.at[pl.ds(n + 8, 8)], (up, left)),
            (last_col.at[pl.ds(0, 8)], to_right.at[pl.ds(n + 8, 8)], (up, right)),
            (first_col.at[pl.ds(n - 8, 8)], to_left.at[pl.ds(0, 8)], (down, left)),
            (last_col.at[pl.ds(n - 8, 8)], to_right.at[pl.ds(0, 8)], (down, right)),
            (first_col, to_left.at[pl.ds(8, n)], (row, left)),
            (last_col, to_right.at[pl.ds(8, n)], (row, right)),
            (first_row, buf.at[b, n + 1, :, lanes], (up, col)),
            (last_row, buf.at[b, 0, :, lanes], (down, col)),
        ]
        rows = sum(math.prod(src.shape) * jnp.dtype(src.dtype).itemsize for src, _, _ in plan) // (4 * chans)
        every = table.at[pl.ds(0, rows)]
        return ([remote(src, dst, h_ssem.at[at], h_rsem.at[at], who) for src, dst, who in plan],
                remote(every, every, h_ssem.at[at], h_rsem.at[at], (row, twin)))

    def send(copies):
        for c in copies[0]:
            c.start()
        sending.append(copies[1])

    def arrive(copies, b, buf, n, lo, hi, rc):
        copies[1].wait_recv()
        nothing = jnp.zeros((buf.shape[2], hi - lo), buf.dtype)

        @pl.when(row == 0)
        def _():
            buf[b, 0, :, lo:hi] = nothing
            rc[b, :, 0:8, :] = jnp.zeros((2, 8, rc.shape[3]), f32)

        @pl.when(row == nr - 1)
        def _():
            buf[b, n + 1, :, lo:hi] = nothing
            rc[b, :, n + 8 : n + 16, :] = jnp.zeros((2, 8, rc.shape[3]), f32)

        @pl.when(col == 0)
        def _():
            rc[b, 0] = jnp.zeros(rc.shape[2:], f32)

        @pl.when(col == nc - 1)
        def _():
            rc[b, 1] = jnp.zeros(rc.shape[2:], f32)

    def widen_fine(buf, b, rc):
        before, after = rc[b, 0, 7 : 7 + tall + 2, :], rc[b, 1, 7 : 7 + tall + 2, :]
        odd = buf[b, :, :, 2 * chans : 3 * chans].astype(f32)
        buf[b, :, :, 0:chans] = shifted(odd, before, 1).astype(bf16)
        even = buf[b, :, :, chans : 2 * chans].astype(f32)
        buf[b, :, :, 3 * chans : 4 * chans] = shifted(even, after, -1).astype(bf16)

    def widen_coarse(buf, b, rc):
        wide_by = rc.shape[3]
        before, after = rc[b, 0, 7 : 7 + low + 2, :], rc[b, 1, 7 : 7 + low + 2, :]
        mid = buf[b, :, :, wide_by : 2 * wide_by].astype(f32)
        buf[b, :, :, 0:wide_by] = shifted(mid, before, 1).astype(bf16)
        buf[b, :, :, 2 * wide_by : 3 * wide_by] = shifted(mid, after, -1).astype(bf16)

    def columns_fine(buf, b, sc):
        sc[b, 0] = buf[b, 1 : tall + 1, 0:16, chans : 2 * chans].astype(f32)[:, 0, :]
        sc[b, 1] = buf[b, 1 : tall + 1, half - 16 : half, 2 * chans : 3 * chans].astype(f32)[:, 15, :]

    def split_latents(b):
        V[b, 1 : tall + 1, :, chans : 3 * chans] = lat[b].reshape(tall, half, 2 * chans)

    def split_cotangent(b):
        def one(k, _):
            rows = pl.ds(k * 16, 16)
            both = cot[b, rows].reshape(16, half, 2 * chans)
            C2[b, rows] = both
            total = both.astype(f32).reshape(8, 2, half, 2 * chans).sum(axis=1)
            total = total[:, :, :chans] + total[:, :, chans:]
            upper = total.astype(bf16)
            rest = (total - upper.astype(f32)).astype(bf16)
            UG[b, pl.ds(k * 8, 8)] = jnp.concatenate([upper, rest], -1)
            return 0

        lax.fori_loop(0, tall // 16, one, 0)

    def prepare_forward():
        w_fwd[...] = jnp.zeros(w_fwd.shape, bf16)
        for i in range(3):
            base = i * 4 * chans
            for part in range(2):
                for j in range(3):
                    at = base + (part + j) * chans
                    w_fwd[at : at + chans, part * chans : (part + 1) * chans] = kfine[i, j]

    def prepare_back():
        w_back[...] = jnp.zeros(w_back.shape, bf16)
        for i in range(3):
            for j in range(3):
                turned = kfine[i, j].T
                for part in range(2):
                    at = i * 4 * chans + (part + 2 - j) * chans
                    w_back[at : at + chans, part * chans : (part + 1) * chans] = turned
                at = (i * 3 + 2 - j) * 2 * chans
                wc_back[at : at + 2 * chans, :] = kcoarse[i, j].T

    def prepare_lift():
        turned = lift[...].T
        upper = turned.astype(bf16)
        lift_hi[0:chans, :] = upper
        lift_hi[chans : 2 * chans, :] = upper
        lift_lo[...] = (turned - upper.astype(f32)).astype(bf16)

    def lift_back(b):
        ug = UG[b].reshape(low * half, 2 * chans)
        CB[b] = dot(ug, lift_hi[...]) + dot(ug[:, :chans], lift_lo[...])

    def forward_fine(b):
        embedding = table[pl.ds(times[b], 1), :]
        embedding = jnp.concatenate([embedding, embedding], -1)
        step = 64

        def one(k, _):
            taps = [V[b, pl.ds(k * step + i, step)].reshape(step * half, 4 * chans) for i in range(3)]
            pre = dot(jnp.concatenate(taps, -1), w_fwd[...]) + embedding
            s = sigmoid(pre)
            hidden = pre * s
            SL[b, pl.ds(k * step, step)] = (s + hidden * (1.0 - s)).reshape(step, half, 2 * chans)
            hidden = hidden.astype(bf16).astype(f32).reshape(step // 2, 2, half, 2 * chans).sum(axis=1)
            pooled = 0.25 * (hidden[:, :, :chans] + hidden[:, :, chans:])
            PO[b, pl.ds(k * (step // 2) + 1, step // 2), :, chans : 2 * chans] = pooled.astype(bf16)
            return 0

        lax.fori_loop(0, tall // step, one, 0)

    def border_columns(buf, b, n):
        strips = []
        for at in (0, 15):
            lo = at // 15 * (half - 16)
            strip = buf[b, :, lo : lo + 16, :].astype(f32)[:, at, :]
            strips.append(jnp.concatenate([strip[i : i + n] for i in range(3)], -1).astype(bf16))
        return strips

    def border_rows(buf, b, first, rows):
        taps = [buf[b, first + i : first + i + rows].reshape(rows * half, buf.shape[3]) for i in range(3)]
        return jnp.concatenate(taps, -1)

    def fine_border(b):
        embedding = table[pl.ds(times[b], 1), :]
        embedding = jnp.concatenate([embedding, embedding], -1)
        taps = border_columns(V, b, tall) + [border_rows(V, b, 0, 2), border_rows(V, b, tall - 2, 2)]
        pre = dot(jnp.concatenate(taps, 0), w_fwd[...]) + embedding
        hidden = (pre * sigmoid(pre)).astype(bf16).astype(f32)
        across = hidden[: 2 * tall].reshape(2 * low, 2, 2 * chans).sum(axis=1)
        across = (0.25 * (across[:, :chans] + across[:, chans:])).astype(bf16).astype(f32)
        sc_p[b, 0], sc_p[b, 1] = across[:low], across[low:]
        along = hidden[2 * tall :].reshape(2, 2, half, 2 * chans).sum(axis=1)
        er_p[b] = (0.25 * (along[:, :, :chans] + along[:, :, chans:])).astype(bf16)

    def coarse_border(b):
        taps = border_columns(PO, b, low) + [border_rows(PO, b, 0, 1), border_rows(PO, b, low - 1, 1)]
        pre = dot(jnp.concatenate(taps, 0), kcoarse[...].reshape(9 * chans, 2 * chans))
        s = sigmoid(pre)
        back = CB[b].reshape(low, half, 2 * chans)
        back = [back[:, 0, :], back[:, half - 1, :], back[0], back[low - 1]]
        grad = jnp.concatenate(back, 0) * (s + pre * s * (1.0 - s))
        grad = grad.astype(bf16)
        sc_c[b, 0], sc_c[b, 1] = grad[:low].astype(f32), grad[low : 2 * low].astype(f32)
        er_c[b, 0], er_c[b, 1] = grad[2 * low : 2 * low + half], grad[2 * low + half :]

    def forward_coarse(b):
        step = 32

        def one(k, _):
            flat = step * half
            taps = [PO[b, pl.ds(k * step + i, step)].reshape(flat, 3 * chans) for i in range(3)]
            weights = kcoarse[...].reshape(9 * chans, 2 * chans)
            pre = dot(jnp.concatenate(taps, -1), weights)
            s = sigmoid(pre)
            act = pre * s
            here = pl.ds(pl.multiple_of(k * flat, flat), flat)
            ACT[b, here, :] = act.astype(bf16)
            grad = (CB[b, here, :] * (s + act * (1.0 - s))).astype(bf16)
            GC[b, pl.ds(k * step + 1, step), :, 2 * chans : 4 * chans] = grad.reshape(step, half, 2 * chans)
            return 0

        lax.fori_loop(0, low // step, one, 0)

    def backward_coarse(b):
        step = 32

        def one(k, total):
            flat = step * half
            taps = [GC[b, pl.ds(k * step + 2 - i, step)].reshape(flat, 6 * chans) for i in range(3)]
            pooled = 0.25 * dot(jnp.concatenate(taps, -1), wc_back[...])
            pooled = pooled.reshape(step, 1, half, chans)
            pooled = jnp.concatenate([pooled, pooled], -1)
            rows = pl.ds(k * 2 * step, 2 * step)
            direct = C2[b, rows].astype(f32).reshape(step, 2, half, 2 * chans)
            slope = SL[b, rows].reshape(step, 2, half, 2 * chans)
            grad = ((direct + pooled) * slope).astype(bf16)
            G[b, pl.ds(k * 2 * step + 1, 2 * step), :, chans : 3 * chans] = grad.reshape(2 * step, half, 2 * chans)
            return total + grad.astype(f32).reshape(2 * flat // 8, 8, 2 * chans).sum(axis=0)

        total = lax.fori_loop(0, low // step, one, jnp.zeros((8, 2 * chans), f32))
        total = total[:, :chans] + total[:, chans:]
        return total.sum(axis=0, keepdims=True)

    stores = []

    def backward_fine(b, part, parts):
        step = 32

        def one(k, _):
            taps = [G[b, pl.ds(k * step + 2 - i, step)].reshape(step * half, 4 * chans) for i in range(3)]
            grad = dot(jnp.concatenate(taps, -1), w_back[...]).astype(bf16)
            OUT[b, pl.ds(k * step, step)] = grad.reshape(step, 2 * half, chans)
            return 0

        each = tall // step // parts
        lax.fori_loop(part * each, (part + 1) * each, one, 0)
        rows = pl.ds(part * each * step, each * step)
        stores.append(pltpu.make_async_copy(OUT.at[b, rows], grad_out.at[b, rows], out_sem.at[len(stores)]))
        stores[-1].start()

    class Reduce:
        def __init__(self, mine, first, part, second, owned, full, ssem, rsem):
            self.refs = mine, first, part, second, owned, full
            self.ssem, self.rsem = ssem, rsem
            self.share, self.half = chans // nr, mine.shape[0] // 2
            self.peers = first.shape[0] - 1

        def all_of(self, phase):
            every = self.refs[3].at[pl.ds(0, pairs - 1)] if phase == 2 else self.refs[1].at[pl.ds(1, self.peers)]
            return remote(every, every, self.ssem.at[phase], self.rsem.at[phase], (row, twin))

        def rows_of(self, peer):
            return pl.ds(pl.multiple_of(peer * self.share, self.share), self.share)

        def chunk(self, ref, owner_core, peer):
            return ref.at[pl.ds(owner_core * self.half, self.half), self.rows_of(peer)]

        def copy1(self, d, to_core):
            mine, first = self.refs[:2]
            peer, flip = lax.rem(row + d, nr), lax.rem(core + to_core, 2)
            return remote(self.chunk(mine, to_core, peer), first.at[2 * d + flip],
                          self.ssem.at[1], self.rsem.at[1], (peer, 2 * pair + to_core))

        def scatter(self, to_core):
            pl.when(core != to_core)(self.copy1(0, to_core).start)
            for d in range(1, nr):
                self.copy1(d, to_core).start()

        def copy2(self, d):
            _, _, part, second = self.refs[:4]
            return remote(part, second.at[pair], self.ssem.at[2], self.rsem.at[2],
                          (row, lax.rem(pair + d, pairs) * 2 + core))

        def cross(self):
            mine, first, part, second = self.refs[:4]
            self.all_of(1).wait_recv()
            total = mine[pl.ds(core * self.half, self.half), self.rows_of(row), :].astype(f32)
            for at in range(1, 2 * nr):
                total = total + first[at].astype(f32)
            part[...] = total.astype(bf16)
            second[pair] = total.astype(bf16)
            for d in range(1, pairs):
                self.copy2(d).start()

        def copy3(self, d, flip):
            owned, full = self.refs[4:]
            peer = lax.rem(row + d, nr)
            return remote(owned, self.chunk(full, core, row), self.ssem.at[3], self.rsem.at[3],
                          (peer, twin if flip else col))

        def collect(self):
            second, owned, full = self.refs[3:]
            self.all_of(2).wait_recv()
            total = second[0].astype(f32)
            for at in range(1, pairs):
                total = total + second[at].astype(f32)
            owned[...] = total.astype(bf16)
            full[pl.ds(core * self.half, self.half), self.rows_of(row), :] = total.astype(bf16)

        def gather(self):
            self.collect()
            for at in range(1, 2 * nr):
                self.copy3(at // 2, at % 2).start()

        def finish(self):
            self.all_of(3).wait_recv()
            for phase in range(1, 4):
                self.all_of(phase).wait_send()

    class ReduceByChip(Reduce):
        def __init__(self, theirs, mixed, *rest):
            super().__init__(*rest)
            self.theirs, self.mixed = theirs, mixed

        def copy0(self):
            give = self.refs[0].at[pl.ds((1 - core) * self.half, self.half)]
            return remote(give, self.theirs, self.ssem.at[0], self.rsem.at[0], (row, twin))

        def copy1(self, d):
            peer = lax.rem(row + d, nr)
            return remote(self.mixed.at[:, self.rows_of(peer)], self.refs[1].at[d],
                          self.ssem.at[1], self.rsem.at[1], (peer, col))

        def scatter(self):
            self.copy0().start()

        def scatter_rows(self):
            self.copy0().wait_recv()
            total = self.refs[0][pl.ds(core * self.half, self.half)] + self.theirs[...]
            self.mixed[...] = total.astype(bf16)
            for d in range(1, nr):
                self.copy1(d).start()

        def cross(self):
            _, first, part, second = self.refs[:4]
            self.all_of(1).wait_recv()
            total = self.mixed[:, self.rows_of(row), :].astype(f32)
            for d in range(1, nr):
                total = total + first[d].astype(f32)
            part[...] = total.astype(bf16)
            second[pair] = total.astype(bf16)
            for d in range(1, pairs):
                self.copy2(d).start()

        def gather(self):
            self.collect()
            for d in range(1, nr):
                self.copy3(d, 0).start()

        def copy4(self):
            done = self.refs[5].at[pl.ds(core * self.half, self.half)]
            return remote(done, done, self.ssem.at[4], self.rsem.at[4], (row, twin))

        def gather_cores(self):
            self.all_of(3).wait_recv()
            self.copy4().start()

        def finish(self):
            self.copy4().wait()
            self.copy0().wait_send()
            for phase in range(1, 4):
                self.all_of(phase).wait_send()

    sum_a = ReduceByChip(a_theirs, a_mixed, a_send, a_r1, a_s2, a_r2, a_t, a_f, a_ssem, a_rsem)
    sum_b = Reduce(b_send, b_r1, b_s2, b_r2, b_t, b_f, b_ssem, b_rsem)

    ex_v = [(b, V, tall, chans, 3 * chans) for b in range(count)]
    ex_p = [(b, PO, low, chans, 2 * chans) for b in range(count)]
    ex_c = [(b, GC, low, 2 * chans, 4 * chans) for b in range(count)]
    ex_g = [(b, G, tall, chans, 3 * chans) for b in range(count)]
    loads["lat0"].wait()
    split_latents(0)
    columns_fine(V, 0, sc_v)
    pl.semaphore_wait(barrier, len(partners))
    moving_v = [exchange(0, *ex_v[b], sc_v, rc_v) for b in range(count)]
    send(moving_v[0])
    loads["lat1"].wait()
    split_latents(1)
    columns_fine(V, 1, sc_v)
    send(moving_v[1])
    load("table", table_in, table)
    load("cot0", cot_in.at[0], cot.at[0])
    load("cot1", cot_in.at[1], cot.at[1])
    load("lift", lift_in, lift)
    load("kcoarse", coarse_in, kcoarse)
    loads["kfine"].wait()
    prepare_forward()
    loads["cot0"].wait()
    split_cotangent(0)
    loads["cot1"].wait()
    split_cotangent(1)
    loads["lift"].wait()
    prepare_lift()
    lift_back(0)
    lift_back(1)
    loads["kcoarse"].wait()
    prepare_back()
    loads["table"].wait()
    loads["times"].wait()

    moving_p = [exchange(1, *ex_p[b], sc_p, rc_p, er_p) for b in range(count)]
    for b in range(count):
        arrive(moving_v[b], *ex_v[b], rc_v)
        widen_fine(V, b, rc_v)
        fine_border(b)
        send(moving_p[b])
    for b in range(count):
        forward_fine(b)

    moving_c = [exchange(2, *ex_c[b], sc_c, rc_c, er_c) for b in range(count)]
    for b in range(count):
        arrive(moving_p[b], *ex_p[b], rc_p)
        widen_coarse(PO, b, rc_p)
        coarse_border(b)
        send(moving_c[b])
    for b in range(count):
        forward_coarse(b)

    lifted = jnp.zeros((2 * chans, 2 * chans), f32)
    for b in range(count):
        lifted = lifted + outer(ACT[b], UG[b].reshape(low * half, 2 * chans))
    lifted = lifted[:, :chans] + lifted[:, chans:]
    a_send[9, :, 0:chans] = lifted[:chans]
    a_send[9, :, chans : 2 * chans] = lifted[chans:]
    for i in range(3):
        kernel_grad = jnp.zeros((2 * chans, 3 * chans), f32)
        for b in range(count):
            grad = GC[b, 1 : low + 1, :, 2 * chans : 4 * chans].reshape(low * half, 2 * chans)
            kernel_grad = kernel_grad + outer(grad, PO[b, i : i + low].reshape(low * half, 3 * chans))
        for j in range(3):
            a_send[3 * i + j] = kernel_grad[:, j * chans : (j + 1) * chans].T
    sum_a.scatter()

    moving_g = [exchange(3, *ex_g[b], sc_g, rc_g) for b in range(count)]
    sums = []
    for b in range(count):
        arrive(moving_c[b], *ex_c[b], rc_c)
        widen_coarse(GC, b, rc_c)
        sums.append(backward_coarse(b))
        columns_fine(G, b, sc_g)
        send(moving_g[b])
        if b == 0:
            sum_a.scatter_rows()

    for i in range(3):
        kernel_grad = jnp.zeros((2 * chans, 4 * chans), f32)
        for b in range(count):
            grad = G[b, 1 : tall + 1, :, chans : 3 * chans].reshape(tall * half, 2 * chans)
            kernel_grad = kernel_grad + outer(grad, V[b, i : i + tall].reshape(tall * half, 4 * chans))
        for j in range(3):
            both = kernel_grad[:chans, j * chans : (j + 1) * chans]
            both = both + kernel_grad[chans:, (j + 1) * chans : (j + 2) * chans]
            b_send[3 * i + j] = both.astype(bf16)
        if i == 1:
            sum_b.scatter(0)
    b_send[9] = jnp.zeros(b_send.shape[1:], bf16)
    sum_b.scatter(1)

    l_send[...] = jnp.concatenate(sums + [jnp.zeros((8 - count, chans), f32)], 0)
    l_moving = [
        remote(l_send, l_r1.at[2 * row + core], l_ssem.at[0], l_rsem.at[0],
               (lax.rem(row + at // 2, nr), twin if at % 2 else col))
        for at in range(1, 2 * nr)
    ]
    every = l_r1.at[pl.ds(0, 2 * nr - 1)]
    l_moving = l_moving, remote(every, every, l_ssem.at[0], l_rsem.at[0], (row, twin))
    send(l_moving)
    l_r1[2 * row + core] = l_send[...]

    arrive(moving_g[0], *ex_g[0], rc_g)
    widen_fine(G, 0, rc_g)
    backward_fine(0, 0, 2)
    backward_fine(0, 1, 2)
    sum_a.cross()
    sum_b.cross()
    l_moving[1].wait_recv()
    total = l_r1[0]
    for at in range(1, 2 * nr):
        total = total + l_r1[at]
    l_s2[...] = total
    l_r2[pair] = total
    l_moving2 = [
        remote(l_s2, l_r2.at[pair], l_ssem.at[1], l_rsem.at[1],
               (row, lax.rem(pair + d, pairs) * 2 + core))
        for d in range(1, pairs)
    ]
    every = l_r2.at[pl.ds(0, pairs - 1)]
    l_moving2 = l_moving2, remote(every, every, l_ssem.at[1], l_rsem.at[1], (row, twin))
    send(l_moving2)

    arrive(moving_g[1], *ex_g[1], rc_g)
    widen_fine(G, 1, rc_g)
    backward_fine(1, 0, 2)
    backward_fine(1, 1, 2)
    sum_a.gather()
    sum_b.gather()
    sum_a.gather_cores()

    l_moving2[1].wait_recv()
    total = l_r2[0]
    for d in range(1, pairs):
        total = total + l_r2[d]
    l_send_done = pltpu.make_async_copy(l_f, l_out, out_sem.at[len(stores)])
    l_f[...] = total
    l_send_done.start()
    stores.append(l_send_done)
    sum_a.finish()
    stores.append(pltpu.make_async_copy(a_f, a_out, out_sem.at[len(stores)]))
    stores[-1].start()
    for c in sending:
        c.wait_send()
    sum_b.finish()
    stores.append(pltpu.make_async_copy(b_f, b_out, out_sem.at[len(stores)]))
    stores[-1].start()
    for c in stores:
        c.wait()


def finishing(
    factor, parts, times_in, grad_in, a_in, b_in, l_in, grad_out, fine_out, coarse_out, lift_out, table_out,
    times, g16, a16, b16, l32, g32, fine, coarse, lift, table, in_sem, out_sem,
):
    count, tall, chans = g16.shape[0], g16.shape[1], g16.shape[3]
    each = tall // parts
    pieces = [(b, pl.ds(p * each, each)) for b in range(count) for p in range(parts)]
    loads = [pltpu.make_async_copy(grad_in.at[b, rows], g16.at[b, rows], in_sem.at[4 + at])
             for at, (b, rows) in enumerate(pieces)]
    loads += [pltpu.make_async_copy(times_in, times, in_sem.at[3]), pltpu.make_async_copy(l_in, l32, in_sem.at[0]), pltpu.make_async_copy(b_in, b16, in_sem.at[1]),
              pltpu.make_async_copy(a_in, a16, in_sem.at[2])]
    for c in loads:
        c.start()
    stores = []

    def store(src, dst):
        stores.append(pltpu.make_async_copy(src, dst, out_sem.at[len(stores)]))
        stores[-1].start()

    for at, (b, rows) in enumerate(pieces):
        loads[at].wait()
        g32[b, rows] = g16[b, rows].astype(f32)
        store(g32.at[b, rows], grad_out.at[b, rows])
    loads[-4].wait()
    loads[-3].wait()
    total = factor * l32[...]
    ids = lax.broadcasted_iota(jnp.int32, table.shape, 0)
    placed = jnp.zeros(table.shape, f32)
    for b in range(count):
        placed = placed + jnp.where(ids == times[b], total[b : b + 1, :], 0.0)
    table[...] = placed
    store(table, table_out)
    loads[-2].wait()
    for t in range(9):
        fine[t // 3, t % 3] = factor * b16[t].astype(f32).T
    store(fine, fine_out)
    loads[-1].wait()
    for t in range(9):
        coarse[t // 3, t % 3] = factor * a16[t].astype(f32)
    store(coarse, coarse_out)
    lift[0:chans, :] = factor * a16[9, :, 0:chans].astype(f32)
    lift[chans : 2 * chans, :] = factor * a16[9, :, chans : 2 * chans].astype(f32)
    store(lift, lift_out)
    for c in stores:
        c.wait()


def solution(mesh):
    nr, nc = mesh.shape["row"], mesh.shape["col"]

    def body(latents, timesteps, time_table, conv_fine, conv_coarse, lift, cotangent):
        count, tall, broad, chans = latents.shape
        half, low = broad // 2, tall // 2
        share, pairs = chans // nr, nc // 2
        factor = 1.0 / math.sqrt(count * tall * broad * nr * nc)
        vm = pltpu.VMEM
        dma = pltpu.SemaphoreType.DMA
        hbm = pl.BlockSpec(memory_space=pl.ANY)

        def reducer(wide, peers, kind):
            return [
                vm((10, chans, wide), kind),
                vm((peers, 5, share, wide), bf16),
                vm((5, share, wide), bf16),
                vm((pairs, 5, share, wide), bf16),
                vm((5, share, wide), bf16),
                vm((10, chans, wide), bf16),
            ]

        def columns(n, wide):
            return [vm((count, 2, n, wide), f32), vm((count, 2, n + 16, wide), f32)]

        scratch = [
            pltpu.SMEM(timesteps.shape, jnp.int32), vm(latents.shape, bf16), vm(cotangent.shape, bf16), vm(time_table.shape, f32),
            vm(conv_fine.shape, bf16), vm(conv_coarse.shape, bf16), vm(lift.shape, f32),
            vm((12 * chans, 2 * chans), bf16), vm((12 * chans, 2 * chans), bf16), vm((18 * chans, chans), bf16),
            vm((2 * chans, 2 * chans), bf16), vm((chans, 2 * chans), bf16),
            vm((count, tall + 2, half, 4 * chans), bf16),
            vm((count, tall, half, 2 * chans), bf16),
            vm((count, tall, half, 2 * chans), f32),
            vm((count, low + 2, half, 3 * chans), bf16),
            vm((count, low, half, 2 * chans), bf16),
            vm((count, low * half, 2 * chans), f32),
            vm((count, low * half, 2 * chans), bf16),
            vm((count, low + 2, half, 6 * chans), bf16),
            vm((count, tall + 2, half, 4 * chans), bf16),
            vm(latents.shape, bf16),
            *columns(tall, chans), *columns(low, chans), *columns(low, 2 * chans), *columns(tall, chans),
            vm((count, 2, half, chans), bf16), vm((count, 2, half, 2 * chans), bf16),
            vm((5, chans, 2 * chans), f32), vm((5, chans, 2 * chans), bf16),
            *reducer(2 * chans, nr, f32), *reducer(chans, 2 * nr, bf16),
            vm((8, chans), f32), vm((2 * nr, 8, chans), f32), vm((8, chans), f32), vm((pairs, 8, chans), f32),
            vm((8, chans), f32),
        ]
        scratch += [dma((9,)), dma((7,)), dma((4 * count,)), dma((4 * count,)), dma((5,)), dma((5,)),
                    dma((5,)), dma((5,)), dma((2,)), dma((2,))]
        shape = jax.ShapeDtypeStruct
        grad, sum_a, sum_b, sum_l = pl.pallas_call(
            functools.partial(kernel, (nr, nc)),
            out_shape=[shape(latents.shape, bf16), shape((10, chans, 2 * chans), bf16),
                       shape((10, chans, chans), bf16), shape((8, chans), f32)],
            in_specs=[hbm] * 7,
            out_specs=[hbm] * 4,
            scratch_shapes=scratch,
            compiler_params=pltpu.CompilerParams(
                collective_id=0, has_side_effects=True, vmem_limit_bytes=60 * 2**20),
        )(timesteps, latents, cotangent, time_table, conv_fine, conv_coarse, lift)

        parts = 4
        results = [latents.shape, conv_fine.shape, conv_coarse.shape, lift.shape, time_table.shape]
        return pl.pallas_call(
            functools.partial(finishing, factor, parts),
            out_shape=[shape(s, f32) for s in results],
            in_specs=[hbm] * 5,
            out_specs=[hbm] * 5,
            scratch_shapes=[
                pltpu.SMEM(timesteps.shape, jnp.int32), vm(latents.shape, bf16), vm(sum_a.shape, bf16), vm(sum_b.shape, bf16), vm(sum_l.shape, f32),
                *[vm(s, f32) for s in results], dma((4 + count * parts,)), dma((4 + count * parts,))],
            compiler_params=pltpu.CompilerParams(vmem_limit_bytes=60 * 2**20),
        )(timesteps, grad, sum_a, sum_b, sum_l)

    in_specs = (P(None, "row", "col", None), P(), P(), P(), P(), P(), P(None, "row", "col", None))
    out_specs = (P(None, "row", "col", None), P(), P(), P(), P())
    return jax.shard_map(body, mesh=mesh, in_specs=in_specs, out_specs=out_specs, check_vma=False)
```

```python
import functools
import math

import jax
import jax.numpy as jnp
from jax import lax
from jax.experimental import pallas as pl
from jax.experimental.pallas import tpu as pltpu
from jax.sharding import PartitionSpec as P

MESH = pl.DeviceIdType.MESH
f32 = jnp.float32
bf16 = jnp.bfloat16


def dot(a, b):
    return jnp.dot(a, b, preferred_element_type=f32)


def outer(a, b):
    return lax.dot_general(a, b, (((0,), (0,)), ((), ())), preferred_element_type=f32)


def sigmoid(v):
    return 0.5 + 0.5 * jnp.tanh(0.5 * v)


def shifted(v, column, step):
    n = v.shape[1]
    ids = lax.broadcasted_iota(jnp.int32, v.shape, 1)
    edge = 0 if step == 1 else n - 1
    return jnp.where(ids == edge, column[:, None, :], pltpu.roll(v, step % n, 1))


def kernel(
    sizes,
    times_in, lat_in, cot_in, table_in, fine_in, coarse_in, lift_in,
    grad_out, a_out, b_out, l_out,
    times, lat, cot, table, kfine, kcoarse, lift,
    w_fwd, w_back, wc_back, lift_hi, lift_lo,
    V, C2, SL, PO, UG, CB, ACT, GC, G, OUT,
    sc_v, rc_v, sc_p, rc_p, sc_c, rc_c, sc_g, rc_g, er_p,
    a_theirs, a_mixed, a_send, a_r1, a_s2, a_r2, a_t, a_f,
    b_send, b_r1, b_s2, b_r2, b_t, b_f,
    l_send, l_r1, l_s2, l_r2, l_f,
    in_sem, out_sem, h_ssem, h_rsem, a_ssem, a_rsem, b_ssem, b_rsem, l_ssem, l_rsem,
):
    nr, nc = sizes
    pairs = nc // 2
    row, col = lax.axis_index("row"), lax.axis_index("col")
    core, pair = lax.rem(col, 2), col // 2
    twin = col + 1 - 2 * core
    up, down = lax.rem(row + nr - 1, nr), lax.rem(row + 1, nr)
    left, right = lax.rem(col + nc - 1, nc), lax.rem(col + 1, nc)
    other = jnp.where(core == 0, left, right)
    count, tall, half = C2.shape[0], C2.shape[1], C2.shape[2]
    low = tall // 2
    chans = lat.shape[3]

    barrier = pltpu.get_barrier_semaphore()
    partners = [(lax.rem(row + d, nr), col) for d in range(1, nr)]
    partners += [(lax.rem(row + d, nr), twin) for d in range(nr)]
    partners += [(row, lax.rem(pair + d, pairs) * 2 + core) for d in range(1, pairs)]
    partners += [(up, other), (row, other), (down, other)]
    for who in partners:
        pl.semaphore_signal(barrier, inc=1, device_id=who, device_id_type=MESH)

    loads = {}

    def load(name, src, dst):
        loads[name] = pltpu.make_async_copy(src, dst, in_sem.at[len(loads)])
        loads[name].start()

    load("lat0", lat_in.at[0], lat.at[0])
    load("lat1", lat_in.at[1], lat.at[1])
    load("kfine", fine_in, kfine)
    load("times", times_in, times)

    sending = []

    def remote(src, dst, ssem, rsem, who):
        return pltpu.make_async_remote_copy(
            src_ref=src, dst_ref=dst, send_sem=ssem, recv_sem=rsem, device_id=who, device_id_type=MESH)

    def exchange(kind, b, buf, n, lo, hi, sc, rc, edges=None):
        at = kind * count + b
        first_col, last_col = sc.at[b, 0], sc.at[b, 1]
        to_left, to_right = rc.at[b, 1], rc.at[b, 0]
        lanes = pl.ds(lo, hi - lo)
        first_row, last_row = buf.at[b, 1, :, lanes], buf.at[b, n, :, lanes]
        if edges is not None:
            first_row, last_row = edges.at[b, 0], edges.at[b, 1]
        plan = [
            (first_col.at[pl.ds(0, 8)], to_left.at[pl.ds(n + 8, 8)], (up, left)),
            (last_col.at[pl.ds(0, 8)], to_right.at[pl.ds(n + 8, 8)], (up, right)),
            (first_col.at[pl.ds(n - 8, 8)], to_left.at[pl.ds(0, 8)], (down, left)),
            (last_col.at[pl.ds(n - 8, 8)], to_right.at[pl.ds(0, 8)], (down, right)),
            (first_col, to_left.at[pl.ds(8, n)], (row, left)),
            (last_col, to_right.at[pl.ds(8, n)], (row, right)),
            (first_row, buf.at[b, n + 1, :, lanes], (up, col)),
            (last_row, buf.at[b, 0, :, lanes], (down, col)),
        ]
        rows = sum(math.prod(src.shape) * jnp.dtype(src.dtype).itemsize for src, _, _ in plan) // (4 * chans)
        every = table.at[pl.ds(0, rows)]
        return ([remote(src, dst, h_ssem.at[at], h_rsem.at[at], who) for src, dst, who in plan],
                remote(every, every, h_ssem.at[at], h_rsem.at[at], (row, twin)))

    def send(copies):
        for c in copies[0]:
            c.start()
        sending.append(copies[1])

    def arrive(copies, b, buf, n, lo, hi, rc):
        copies[1].wait_recv()
        nothing = jnp.zeros((buf.shape[2], hi - lo), buf.dtype)

        @pl.when(row == 0)
        def _():
            buf[b, 0, :, lo:hi] = nothing
            rc[b, :, 0:8, :] = jnp.zeros((2, 8, rc.shape[3]), f32)

        @pl.when(row == nr - 1)
        def _():
            buf[b, n + 1, :, lo:hi] = nothing
            rc[b, :, n + 8 : n + 16, :] = jnp.zeros((2, 8, rc.shape[3]), f32)

        @pl.when(col == 0)
        def _():
            rc[b, 0] = jnp.zeros(rc.shape[2:], f32)

        @pl.when(col == nc - 1)
        def _():
            rc[b, 1] = jnp.zeros(rc.shape[2:], f32)

    def widen_fine(buf, b, rc):
        before, after = rc[b, 0, 7 : 7 + tall + 2, :], rc[b, 1, 7 : 7 + tall + 2, :]
        odd = buf[b, :, :, 2 * chans : 3 * chans].astype(f32)
        buf[b, :, :, 0:chans] = shifted(odd, before, 1).astype(bf16)
        even = buf[b, :, :, chans : 2 * chans].astype(f32)
        buf[b, :, :, 3 * chans : 4 * chans] = shifted(even, after, -1).astype(bf16)

    def widen_coarse(buf, b, rc):
        wide_by = rc.shape[3]
        before, after = rc[b, 0, 7 : 7 + low + 2, :], rc[b, 1, 7 : 7 + low + 2, :]
        mid = buf[b, :, :, wide_by : 2 * wide_by].astype(f32)
        buf[b, :, :, 0:wide_by] = shifted(mid, before, 1).astype(bf16)
        buf[b, :, :, 2 * wide_by : 3 * wide_by] = shifted(mid, after, -1).astype(bf16)

    def columns_fine(buf, b, sc):
        sc[b, 0] = buf[b, 1 : tall + 1, 0:16, chans : 2 * chans].astype(f32)[:, 0, :]
        sc[b, 1] = buf[b, 1 : tall + 1, half - 16 : half, 2 * chans : 3 * chans].astype(f32)[:, 15, :]

    def split_latents(b):
        V[b, 1 : tall + 1, :, chans : 3 * chans] = lat[b].reshape(tall, half, 2 * chans)

    def split_cotangent(b):
        def one(k, _):
            rows = pl.ds(k * 16, 16)
            both = cot[b, rows].reshape(16, half, 2 * chans)
            C2[b, rows] = both
            total = both.astype(f32).reshape(8, 2, half, 2 * chans).sum(axis=1)
            total = total[:, :, :chans] + total[:, :, chans:]
            upper = total.astype(bf16)
            rest = (total - upper.astype(f32)).astype(bf16)
            UG[b, pl.ds(k * 8, 8)] = jnp.concatenate([upper, rest], -1)
            return 0

        lax.fori_loop(0, tall // 16, one, 0)

    def prepare_forward():
        w_fwd[...] = jnp.zeros(w_fwd.shape, bf16)
        for i in range(3):
            base = i * 4 * chans
            for part in range(2):
                for j in range(3):
                    at = base + (part + j) * chans
                    w_fwd[at : at + chans, part * chans : (part + 1) * chans] = kfine[i, j]

    def prepare_back():
        w_back[...] = jnp.zeros(w_back.shape, bf16)
        for i in range(3):
            for j in range(3):
                turned = kfine[i, j].T
                for part in range(2):
                    at = i * 4 * chans + (part + 2 - j) * chans
                    w_back[at : at + chans, part * chans : (part + 1) * chans] = turned
                at = (i * 3 + 2 - j) * 2 * chans
                wc_back[at : at + 2 * chans, :] = kcoarse[i, j].T

    def prepare_lift():
        turned = lift[...].T
        upper = turned.astype(bf16)
        lift_hi[0:chans, :] = upper
        lift_hi[chans : 2 * chans, :] = upper
        lift_lo[...] = (turned - upper.astype(f32)).astype(bf16)

    def lift_back(b):
        ug = UG[b].reshape(low * half, 2 * chans)
        CB[b] = dot(ug, lift_hi[...]) + dot(ug[:, :chans], lift_lo[...])

    def forward_fine(b):
        embedding = table[pl.ds(times[b], 1), :]
        embedding = jnp.concatenate([embedding, embedding], -1)
        step = 32

        def one(k, _):
            taps = [V[b, pl.ds(k * step + i, step)].reshape(step * half, 4 * chans) for i in range(3)]
            pre = dot(jnp.concatenate(taps, -1), w_fwd[...]) + embedding
            s = sigmoid(pre)
            hidden = pre * s
            SL[b, pl.ds(k * step, step)] = (s + hidden * (1.0 - s)).reshape(step, half, 2 * chans)
            hidden = hidden.astype(bf16).astype(f32).reshape(step // 2, 2, half, 2 * chans).sum(axis=1)
            pooled = 0.25 * (hidden[:, :, :chans] + hidden[:, :, chans:])
            PO[b, pl.ds(k * (step // 2) + 1, step // 2), :, chans : 2 * chans] = pooled.astype(bf16)
            return 0

        lax.fori_loop(0, tall // step, one, 0)

    def border_columns(buf, b, n):
        strips = []
        for at in (0, 15):
            lo = at // 15 * (half - 16)
            strip = buf[b, :, lo : lo + 16, :].astype(f32)[:, at, :]
            strips.append(jnp.concatenate([strip[i : i + n] for i in range(3)], -1).astype(bf16))
        return strips

    def border_rows(buf, b, first, rows):
        taps = [buf[b, first + i : first + i + rows].reshape(rows * half, buf.shape[3]) for i in range(3)]
        return jnp.concatenate(taps, -1)

    def fine_border(b):
        embedding = table[pl.ds(times[b], 1), :]
        embedding = jnp.concatenate([embedding, embedding], -1)
        taps = border_columns(V, b, tall) + [border_rows(V, b, 0, 2), border_rows(V, b, tall - 2, 2)]
        pre = dot(jnp.concatenate(taps, 0), w_fwd[...]) + embedding
        hidden = (pre * sigmoid(pre)).astype(bf16).astype(f32)
        across = hidden[: 2 * tall].reshape(2 * low, 2, 2 * chans).sum(axis=1)
        across = (0.25 * (across[:, :chans] + across[:, chans:])).astype(bf16).astype(f32)
        sc_p[b, 0], sc_p[b, 1] = across[:low], across[low:]
        along = hidden[2 * tall :].reshape(2, 2, half, 2 * chans).sum(axis=1)
        er_p[b] = (0.25 * (along[:, :, :chans] + along[:, :, chans:])).astype(bf16)

    def forward_coarse(b):
        step = 32

        def one(k, _):
            flat = step * half
            taps = [PO[b, pl.ds(k * step + i, step)].reshape(flat, 3 * chans) for i in range(3)]
            weights = kcoarse[...].reshape(9 * chans, 2 * chans)
            pre = dot(jnp.concatenate(taps, -1), weights)
            s = sigmoid(pre)
            act = pre * s
            here = pl.ds(pl.multiple_of(k * flat, flat), flat)
            ACT[b, here, :] = act.astype(bf16)
            grad = (CB[b, here, :] * (s + act * (1.0 - s))).astype(bf16)
            GC[b, pl.ds(k * step + 1, step), :, 2 * chans : 4 * chans] = grad.reshape(step, half, 2 * chans)
            return 0

        lax.fori_loop(0, low // step, one, 0)

    def backward_coarse(b):
        step = 32

        def one(k, total):
            flat = step * half
            taps = [GC[b, pl.ds(k * step + 2 - i, step)].reshape(flat, 6 * chans) for i in range(3)]
            pooled = 0.25 * dot(jnp.concatenate(taps, -1), wc_back[...])
            pooled = pooled.reshape(step, 1, half, chans)
            pooled = jnp.concatenate([pooled, pooled], -1)
            rows = pl.ds(k * 2 * step, 2 * step)
            direct = C2[b, rows].astype(f32).reshape(step, 2, half, 2 * chans)
            slope = SL[b, rows].reshape(step, 2, half, 2 * chans)
            grad = ((direct + pooled) * slope).astype(bf16)
            G[b, pl.ds(k * 2 * step + 1, 2 * step), :, chans : 3 * chans] = grad.reshape(2 * step, half, 2 * chans)
            return total + grad.astype(f32).reshape(2 * flat // 8, 8, 2 * chans).sum(axis=0)

        total = lax.fori_loop(0, low // step, one, jnp.zeros((8, 2 * chans), f32))
        total = total[:, :chans] + total[:, chans:]
        return total.sum(axis=0, keepdims=True)

    stores = []

    def backward_fine(b, part, parts):
        step = 32

        def one(k, _):
            taps = [G[b, pl.ds(k * step + 2 - i, step)].reshape(step * half, 4 * chans) for i in range(3)]
            grad = dot(jnp.concatenate(taps, -1), w_back[...]).astype(bf16)
            OUT[b, pl.ds(k * step, step)] = grad.reshape(step, 2 * half, chans)
            return 0

        each = tall // step // parts
        lax.fori_loop(part * each, (part + 1) * each, one, 0)
        rows = pl.ds(part * each * step, each * step)
        stores.append(pltpu.make_async_copy(OUT.at[b, rows], grad_out.at[b, rows], out_sem.at[len(stores)]))
        stores[-1].start()

    class Reduce:
        def __init__(self, mine, first, part, second, owned, full, ssem, rsem):
            self.refs = mine, first, part, second, owned, full
            self.ssem, self.rsem = ssem, rsem
            self.share, self.half = chans // nr, mine.shape[0] // 2
            self.peers = first.shape[0] - 1

        def all_of(self, phase):
            every = self.refs[3].at[pl.ds(0, pairs - 1)] if phase == 2 else self.refs[1].at[pl.ds(1, self.peers)]
            return remote(every, every, self.ssem.at[phase], self.rsem.at[phase], (row, twin))

        def rows_of(self, peer):
            return pl.ds(pl.multiple_of(peer * self.share, self.share), self.share)

        def chunk(self, ref, owner_core, peer):
            return ref.at[pl.ds(owner_core * self.half, self.half), self.rows_of(peer)]

        def copy1(self, d, to_core):
            mine, first = self.refs[:2]
            peer, flip = lax.rem(row + d, nr), lax.rem(core + to_core, 2)
            return remote(self.chunk(mine, to_core, peer), first.at[2 * d + flip],
                          self.ssem.at[1], self.rsem.at[1], (peer, 2 * pair + to_core))

        def scatter(self, to_core):
            pl.when(core != to_core)(self.copy1(0, to_core).start)
            for d in range(1, nr):
                self.copy1(d, to_core).start()

        def copy2(self, d):
            _, _, part, second = self.refs[:4]
            return remote(part, second.at[pair], self.ssem.at[2], self.rsem.at[2],
                          (row, lax.rem(pair + d, pairs) * 2 + core))

        def cross(self):
            mine, first, part, second = self.refs[:4]
            self.all_of(1).wait_recv()
            total = mine[pl.ds(core * self.half, self.half), self.rows_of(row), :].astype(f32)
            for at in range(1, 2 * nr):
                total = total + first[at].astype(f32)
            part[...] = total.astype(bf16)
            second[pair] = total.astype(bf16)
            for d in range(1, pairs):
                self.copy2(d).start()

        def copy3(self, d, flip):
            owned, full = self.refs[4:]
            peer = lax.rem(row + d, nr)
            return remote(owned, self.chunk(full, core, row), self.ssem.at[3], self.rsem.at[3],
                          (peer, twin if flip else col))

        def collect(self):
            second, owned, full = self.refs[3:]
            self.all_of(2).wait_recv()
            total = second[0].astype(f32)
            for at in range(1, pairs):
                total = total + second[at].astype(f32)
            owned[...] = total.astype(bf16)
            full[pl.ds(core * self.half, self.half), self.rows_of(row), :] = total.astype(bf16)

        def gather(self):
            self.collect()
            for at in range(1, 2 * nr):
                self.copy3(at // 2, at % 2).start()

        def finish(self):
            self.all_of(3).wait_recv()
            for phase in range(1, 4):
                self.all_of(phase).wait_send()

    class ReduceByChip(Reduce):
        def __init__(self, theirs, mixed, *rest):
            super().__init__(*rest)
            self.theirs, self.mixed = theirs, mixed

        def copy0(self):
            give = self.refs[0].at[pl.ds((1 - core) * self.half, self.half)]
            return remote(give, self.theirs, self.ssem.at[0], self.rsem.at[0], (row, twin))

        def copy1(self, d):
            peer = lax.rem(row + d, nr)
            return remote(self.mixed.at[:, self.rows_of(peer)], self.refs[1].at[d],
                          self.ssem.at[1], self.rsem.at[1], (peer, col))

        def scatter(self):
            self.copy0().start()

        def scatter_rows(self):
            self.copy0().wait_recv()
            total = self.refs[0][pl.ds(core * self.half, self.half)] + self.theirs[...]
            self.mixed[...] = total.astype(bf16)
            for d in range(1, nr):
                self.copy1(d).start()

        def cross(self):
            _, first, part, second = self.refs[:4]
            self.all_of(1).wait_recv()
            total = self.mixed[:, self.rows_of(row), :].astype(f32)
            for d in range(1, nr):
                total = total + first[d].astype(f32)
            part[...] = total.astype(bf16)
            second[pair] = total.astype(bf16)
            for d in range(1, pairs):
                self.copy2(d).start()

        def gather(self):
            self.collect()
            for d in range(1, nr):
                self.copy3(d, 0).start()

        def copy4(self):
            done = self.refs[5].at[pl.ds(core * self.half, self.half)]
            return remote(done, done, self.ssem.at[4], self.rsem.at[4], (row, twin))

        def gather_cores(self):
            self.all_of(3).wait_recv()
            self.copy4().start()

        def finish(self):
            self.copy4().wait()
            self.copy0().wait_send()
            for phase in range(1, 4):
                self.all_of(phase).wait_send()

    sum_a = ReduceByChip(a_theirs, a_mixed, a_send, a_r1, a_s2, a_r2, a_t, a_f, a_ssem, a_rsem)
    sum_b = Reduce(b_send, b_r1, b_s2, b_r2, b_t, b_f, b_ssem, b_rsem)

    ex_v = [(b, V, tall, chans, 3 * chans) for b in range(count)]
    ex_p = [(b, PO, low, chans, 2 * chans) for b in range(count)]
    ex_c = [(b, GC, low, 2 * chans, 4 * chans) for b in range(count)]
    ex_g = [(b, G, tall, chans, 3 * chans) for b in range(count)]
    loads["lat0"].wait()
    split_latents(0)
    columns_fine(V, 0, sc_v)
    pl.semaphore_wait(barrier, len(partners))
    moving_v = [exchange(0, *ex_v[b], sc_v, rc_v) for b in range(count)]
    send(moving_v[0])
    loads["lat1"].wait()
    split_latents(1)
    columns_fine(V, 1, sc_v)
    send(moving_v[1])
    load("table", table_in, table)
    load("cot0", cot_in.at[0], cot.at[0])
    load("cot1", cot_in.at[1], cot.at[1])
    load("lift", lift_in, lift)
    load("kcoarse", coarse_in, kcoarse)
    loads["kfine"].wait()
    prepare_forward()
    loads["cot0"].wait()
    split_cotangent(0)
    loads["cot1"].wait()
    split_cotangent(1)
    loads["lift"].wait()
    prepare_lift()
    lift_back(0)
    lift_back(1)
    loads["kcoarse"].wait()
    prepare_back()
    loads["table"].wait()
    loads["times"].wait()

    moving_p = [exchange(1, *ex_p[b], sc_p, rc_p, er_p) for b in range(count)]
    for b in range(count):
        arrive(moving_v[b], *ex_v[b], rc_v)
        widen_fine(V, b, rc_v)
        fine_border(b)
        send(moving_p[b])
    for b in range(count):
        forward_fine(b)

    moving_c = [exchange(2, *ex_c[b], sc_c, rc_c) for b in range(count)]
    for b in range(count):
        arrive(moving_p[b], *ex_p[b], rc_p)
        widen_coarse(PO, b, rc_p)
        forward_coarse(b)
        here = slice(2 * chans, 4 * chans)
        sc_c[b, 0] = GC[b, 1 : low + 1, 0:16, here].astype(f32)[:, 0, :]
        sc_c[b, 1] = GC[b, 1 : low + 1, half - 16 : half, here].astype(f32)[:, 15, :]
        send(moving_c[b])

    lifted = jnp.zeros((2 * chans, 2 * chans), f32)
    for b in range(count):
        lifted = lifted + outer(ACT[b], UG[b].reshape(low * half, 2 * chans))
    lifted = lifted[:, :chans] + lifted[:, chans:]
    a_send[9, :, 0:chans] = lifted[:chans]
    a_send[9, :, chans : 2 * chans] = lifted[chans:]
    for i in range(3):
        kernel_grad = jnp.zeros((2 * chans, 3 * chans), f32)
        for b in range(count):
            grad = GC[b, 1 : low + 1, :, 2 * chans : 4 * chans].reshape(low * half, 2 * chans)
            kernel_grad = kernel_grad + outer(grad, PO[b, i : i + low].reshape(low * half, 3 * chans))
        for j in range(3):
            a_send[3 * i + j] = kernel_grad[:, j * chans : (j + 1) * chans].T
    sum_a.scatter()

    moving_g = [exchange(3, *ex_g[b], sc_g, rc_g) for b in range(count)]
    sums = []
    for b in range(count):
        arrive(moving_c[b], *ex_c[b], rc_c)
        widen_coarse(GC, b, rc_c)
        sums.append(backward_coarse(b))
        columns_fine(G, b, sc_g)
        send(moving_g[b])
        if b == 0:
            sum_a.scatter_rows()

    l_send[...] = jnp.concatenate(sums + [jnp.zeros((8 - count, chans), f32)], 0)
    l_moving = [
        remote(l_send, l_r1.at[2 * row + core], l_ssem.at[0], l_rsem.at[0],
               (lax.rem(row + at // 2, nr), twin if at % 2 else col))
        for at in range(1, 2 * nr)
    ]
    every = l_r1.at[pl.ds(0, 2 * nr - 1)]
    l_moving = l_moving, remote(every, every, l_ssem.at[0], l_rsem.at[0], (row, twin))
    send(l_moving)
    l_r1[2 * row + core] = l_send[...]

    for i in range(3):
        kernel_grad = jnp.zeros((2 * chans, 4 * chans), f32)
        for b in range(count):
            grad = G[b, 1 : tall + 1, :, chans : 3 * chans].reshape(tall * half, 2 * chans)
            kernel_grad = kernel_grad + outer(grad, V[b, i : i + tall].reshape(tall * half, 4 * chans))
        for j in range(3):
            both = kernel_grad[:chans, j * chans : (j + 1) * chans]
            both = both + kernel_grad[chans:, (j + 1) * chans : (j + 2) * chans]
            b_send[3 * i + j] = both.astype(bf16)
        if i == 1:
            sum_b.scatter(0)
    b_send[9] = jnp.zeros(b_send.shape[1:], bf16)
    sum_b.scatter(1)

    arrive(moving_g[0], *ex_g[0], rc_g)
    widen_fine(G, 0, rc_g)
    sum_a.cross()
    backward_fine(0, 0, 2)
    backward_fine(0, 1, 2)
    l_moving[1].wait_recv()
    total = l_r1[0]
    for at in range(1, 2 * nr):
        total = total + l_r1[at]
    l_s2[...] = total
    l_r2[pair] = total
    l_moving2 = [
        remote(l_s2, l_r2.at[pair], l_ssem.at[1], l_rsem.at[1],
               (row, lax.rem(pair + d, pairs) * 2 + core))
        for d in range(1, pairs)
    ]
    every = l_r2.at[pl.ds(0, pairs - 1)]
    l_moving2 = l_moving2, remote(every, every, l_ssem.at[1], l_rsem.at[1], (row, twin))
    send(l_moving2)

    arrive(moving_g[1], *ex_g[1], rc_g)
    widen_fine(G, 1, rc_g)
    backward_fine(1, 0, 2)
    sum_b.cross()
    backward_fine(1, 1, 2)
    sum_a.gather()
    sum_b.gather()
    sum_a.gather_cores()

    l_moving2[1].wait_recv()
    total = l_r2[0]
    for d in range(1, pairs):
        total = total + l_r2[d]
    l_send_done = pltpu.make_async_copy(l_f, l_out, out_sem.at[len(stores)])
    l_f[...] = total
    l_send_done.start()
    stores.append(l_send_done)
    sum_a.finish()
    stores.append(pltpu.make_async_copy(a_f, a_out, out_sem.at[len(stores)]))
    stores[-1].start()
    for c in sending:
        c.wait_send()
    sum_b.finish()
    stores.append(pltpu.make_async_copy(b_f, b_out, out_sem.at[len(stores)]))
    stores[-1].start()
    for c in stores:
        c.wait()


def finishing(
    factor, parts, times_in, grad_in, a_in, b_in, l_in, grad_out, fine_out, coarse_out, lift_out, table_out,
    times, g16, a16, b16, l32, g32, fine, coarse, lift, table, in_sem, out_sem,
):
    count, tall, chans = g16.shape[0], g16.shape[1], g16.shape[3]
    each = tall // parts
    pieces = [(b, pl.ds(p * each, each)) for b in range(count) for p in range(parts)]
    loads = [pltpu.make_async_copy(grad_in.at[b, rows], g16.at[b, rows], in_sem.at[4 + at])
             for at, (b, rows) in enumerate(pieces)]
    loads += [pltpu.make_async_copy(times_in, times, in_sem.at[3]), pltpu.make_async_copy(l_in, l32, in_sem.at[0]), pltpu.make_async_copy(b_in, b16, in_sem.at[1]),
              pltpu.make_async_copy(a_in, a16, in_sem.at[2])]
    for c in loads:
        c.start()
    stores = []

    def store(src, dst):
        stores.append(pltpu.make_async_copy(src, dst, out_sem.at[len(stores)]))
        stores[-1].start()

    for at, (b, rows) in enumerate(pieces):
        loads[at].wait()
        g32[b, rows] = g16[b, rows].astype(f32)
        store(g32.at[b, rows], grad_out.at[b, rows])
    loads[-4].wait()
    loads[-3].wait()
    total = factor * l32[...]
    ids = lax.broadcasted_iota(jnp.int32, table.shape, 0)
    placed = jnp.zeros(table.shape, f32)
    for b in range(count):
        placed = placed + jnp.where(ids == times[b], total[b : b + 1, :], 0.0)
    table[...] = placed
    store(table, table_out)
    loads[-2].wait()
    for t in range(9):
        fine[t // 3, t % 3] = factor * b16[t].astype(f32).T
    store(fine, fine_out)
    loads[-1].wait()
    for t in range(9):
        coarse[t // 3, t % 3] = factor * a16[t].astype(f32)
    store(coarse, coarse_out)
    lift[0:chans, :] = factor * a16[9, :, 0:chans].astype(f32)
    lift[chans : 2 * chans, :] = factor * a16[9, :, chans : 2 * chans].astype(f32)
    store(lift, lift_out)
    for c in stores:
        c.wait()


def solution(mesh):
    nr, nc = mesh.shape["row"], mesh.shape["col"]

    def body(latents, timesteps, time_table, conv_fine, conv_coarse, lift, cotangent):
        count, tall, broad, chans = latents.shape
        half, low = broad // 2, tall // 2
        share, pairs = chans // nr, nc // 2
        factor = 1.0 / math.sqrt(count * tall * broad * nr * nc)
        vm = pltpu.VMEM
        dma = pltpu.SemaphoreType.DMA
        hbm = pl.BlockSpec(memory_space=pl.ANY)

        def reducer(wide, peers, kind):
            return [
                vm((10, chans, wide), kind),
                vm((peers, 5, share, wide), bf16),
                vm((5, share, wide), bf16),
                vm((pairs, 5, share, wide), bf16),
                vm((5, share, wide), bf16),
                vm((10, chans, wide), bf16),
            ]

        def columns(n, wide):
            return [vm((count, 2, n, wide), f32), vm((count, 2, n + 16, wide), f32)]

        scratch = [
            pltpu.SMEM(timesteps.shape, jnp.int32), vm(latents.shape, bf16), vm(cotangent.shape, bf16), vm(time_table.shape, f32),
            vm(conv_fine.shape, bf16), vm(conv_coarse.shape, bf16), vm(lift.shape, f32),
            vm((12 * chans, 2 * chans), bf16), vm((12 * chans, 2 * chans), bf16), vm((18 * chans, chans), bf16),
            vm((2 * chans, 2 * chans), bf16), vm((chans, 2 * chans), bf16),
            vm((count, tall + 2, half, 4 * chans), bf16),
            vm((count, tall, half, 2 * chans), bf16),
            vm((count, tall, half, 2 * chans), f32),
            vm((count, low + 2, half, 3 * chans), bf16),
            vm((count, low, half, 2 * chans), bf16),
            vm((count, low * half, 2 * chans), f32),
            vm((count, low * half, 2 * chans), bf16),
            vm((count, low + 2, half, 6 * chans), bf16),
            vm((count, tall + 2, half, 4 * chans), bf16),
            vm(latents.shape, bf16),
            *columns(tall, chans), *columns(low, chans), *columns(low, 2 * chans), *columns(tall, chans),
            vm((count, 2, half, chans), bf16),
            vm((5, chans, 2 * chans), f32), vm((5, chans, 2 * chans), bf16),
            *reducer(2 * chans, nr, f32), *reducer(chans, 2 * nr, bf16),
            vm((8, chans), f32), vm((2 * nr, 8, chans), f32), vm((8, chans), f32), vm((pairs, 8, chans), f32),
            vm((8, chans), f32),
        ]
        scratch += [dma((9,)), dma((7,)), dma((4 * count,)), dma((4 * count,)), dma((5,)), dma((5,)),
                    dma((5,)), dma((5,)), dma((2,)), dma((2,))]
        shape = jax.ShapeDtypeStruct
        grad, sum_a, sum_b, sum_l = pl.pallas_call(
            functools.partial(kernel, (nr, nc)),
            out_shape=[shape(latents.shape, bf16), shape((10, chans, 2 * chans), bf16),
                       shape((10, chans, chans), bf16), shape((8, chans), f32)],
            in_specs=[hbm] * 7,
            out_specs=[hbm] * 4,
            scratch_shapes=scratch,
            compiler_params=pltpu.CompilerParams(
                collective_id=0, has_side_effects=True, vmem_limit_bytes=60 * 2**20),
        )(timesteps, latents, cotangent, time_table, conv_fine, conv_coarse, lift)

        parts = 4
        results = [latents.shape, conv_fine.shape, conv_coarse.shape, lift.shape, time_table.shape]
        return pl.pallas_call(
            functools.partial(finishing, factor, parts),
            out_shape=[shape(s, f32) for s in results],
            in_specs=[hbm] * 5,
            out_specs=[hbm] * 5,
            scratch_shapes=[
                pltpu.SMEM(timesteps.shape, jnp.int32), vm(latents.shape, bf16), vm(sum_a.shape, bf16), vm(sum_b.shape, bf16), vm(sum_l.shape, f32),
                *[vm(s, f32) for s in results], dma((4 + count * parts,)), dma((4 + count * parts,))],
            compiler_params=pltpu.CompilerParams(vmem_limit_bytes=60 * 2**20),
        )(timesteps, grad, sum_a, sum_b, sum_l)

    in_specs = (P(None, "row", "col", None), P(), P(), P(), P(), P(), P(None, "row", "col", None))
    out_specs = (P(None, "row", "col", None), P(), P(), P(), P())
    return jax.shard_map(body, mesh=mesh, in_specs=in_specs, out_specs=out_specs, check_vma=False)
```
